32 devices in a mesh: rep: 8 (over y, x, core), exp: 4 (over z).
Axes of the slice: x: 2, y: 2, z: 4, core: 2. Of those that a mesh axis runs over, the one named last changes fastest.
Arguments:
- tokens: bfloat16 [4096, 2048], P(('rep', 'exp')), may hold values from -6 to 6
- expert_ids: int32 [4096, 1], P(('rep', 'exp')), may hold values from 0 to 3
- norm_gain: float32 [2048], replicated, may hold values from 0.1 to 1.9
- up_weight: bfloat16 [4, 2048, 4096], P('exp', None, 'rep'), may hold values from -0.125 to 0.125
- down_weight: bfloat16 [4, 4096, 2048], P('exp', 'rep'), may hold values from -0.09375 to 0.09375
- cotangent: bfloat16 [4096, 2048], P(('rep', 'exp')), may hold values from -6 to 6
Outputs:
- mixed: bfloat16 [4096, 2048], P(('rep', 'exp'))
- grad_tokens: bfloat16 [4096, 2048], P(('rep', 'exp'))
- grad_up: bfloat16 [4, 2048, 4096], P('exp', None, 'rep')
- grad_down: bfloat16 [4, 4096, 2048], P('exp', 'rep')
- grad_gain: float32 [2048], replicated
The draws below stay inside these ranges and needn't reach their ends.
All inputs are finite; a program needn't handle non-finite values.
Results may differ from the reference program's by a relative error of at most 0.014.
Values may be sent and summed in bfloat16 or wider, within the bound.
No kernel may reach another device: no remote copies, remote signals or barrier semaphores. Data moves between devices by JAX's collectives and lax.ppermute only.
A program may use at most 128 MiB of HBM per device.

```python
import jax
import jax.numpy as jnp
from jax import lax

D = 2048
H = 4096
TOK_DEV = 128
E = 4
CAP = 24
TOKENS = 4096
N_REP = 8
N_EXP = 4


def shard_levels(stream_key, shape, pieces, least, top_value):
    level = 1.0
    for axis_at, shards_of in pieces:
        steps = jax.random.uniform(jax.random.fold_in(jax.random.fold_in(stream_key, 6), axis_at), (shards_of,), jnp.float32, least / len(pieces), top_value / len(pieces))
        level = level * jnp.repeat(jnp.exp(steps), shape[axis_at] // shards_of).reshape((-1,) + (1,) * (len(shape) - 1 - axis_at))
    return level


def different_ones(stream_key, rows, amount, top, lift):
    ranking = jax.random.permutation(jax.random.fold_in(stream_key, 1), amount)
    boost = ranking
    for power in range(3):
        boost = boost * boost // amount
    boost = boost * lift // amount
    lots = jax.random.randint(jax.random.fold_in(stream_key, 2), (rows, amount), 0, 4096) + boost
    holders = jax.random.permutation(jax.random.fold_in(stream_key, 3), rows)[jnp.arange(amount) % rows]
    lots = jnp.where(jnp.arange(rows)[:, None] == holders[None, :], 1 << 14, lots)
    score = lots * amount + jnp.arange(amount)
    return lax.top_k(score.astype(jnp.int32), top)[1].astype(jnp.int32)


def gaussian(own_key, shape, deviation, bound, cuts=(), kind=jnp.bfloat16):
    drawn = deviation * jax.random.normal(own_key, shape, jnp.float32)
    if cuts:
        drawn = drawn * shard_levels(own_key, shape, cuts, -0.22, 0.18)
    return jnp.clip(drawn, -bound, bound).astype(kind)


def setup_inputs(seed: int = 0) -> dict:
    key_of = jax.random.split(jax.random.key(seed), 7)
    return {
        "tokens": gaussian(key_of[0], (TOKENS, D), 1.0, 6.0, ((0, 32),)),
        "expert_ids": different_ones(key_of[1], TOKENS, E, 1, 4096),
        "norm_gain": jnp.clip(1.0 + 0.18 * jax.random.normal(key_of[2], (D,), jnp.float32), 0.1, 1.9),
        "up_weight": gaussian(key_of[3], (E, D, H), D ** -0.5, 0.125, ((0, 4), (2, 8))),
        "down_weight": gaussian(key_of[4], (E, H, D), H ** -0.5, 0.09375, ((0, 4), (1, 8))),
        "cotangent": gaussian(key_of[5], (TOKENS, D), 1.0, 6.0, ((0, 32),)),
    }


gelu_coef = 0.7978845608028654
cubic_coef = 0.044715

def gelu_parts(inputs):
    inner = gelu_coef * (inputs + cubic_coef * inputs * inputs * inputs)
    tangent = jnp.tanh(inner)
    values = 0.5 * inputs * (1.0 + tangent)
    slopes = 0.5 * (1.0 + tangent) + 0.5 * inputs * (1.0 - tangent * tangent) * gelu_coef * (1.0 + 3.0 * cubic_coef * inputs * inputs)
    return (values, slopes)

def reference(tokens, expert_ids, norm_gain, up_weight, down_weight, cotangent):
    devices_all = N_REP * N_EXP
    slot_rows = devices_all * CAP
    hidden_dev = H // N_REP
    wide_tokens = tokens.astype(jnp.float32)
    scales = lax.rsqrt(lax.optimization_barrier(jnp.mean(wide_tokens * wide_tokens, axis=1, keepdims=True)) + 1e-06)
    normed = (wide_tokens * scales * norm_gain).astype(jnp.bfloat16)
    expert_row = expert_ids[:, 0].astype(jnp.int32).reshape(devices_all, TOK_DEV)
    one_hot = (expert_row[:, :, None] == jnp.arange(E, dtype=jnp.int32)[None, None, :]).astype(jnp.int32)
    before = (jnp.cumsum(one_hot, axis=1).astype(jnp.int32) - one_hot) * one_hot
    ranks = lax.optimization_barrier(jnp.sum(before, axis=2)).astype(jnp.int32)
    is_kept = ranks < CAP
    device_ids = jnp.arange(devices_all, dtype=jnp.int32)[:, None]
    slot_of = jnp.where(is_kept, expert_row * slot_rows + device_ids * CAP + ranks, E * slot_rows).astype(jnp.int32).reshape(TOKENS)
    owner = jnp.full((E * slot_rows,), TOKENS, jnp.int32).at[slot_of].set(jnp.arange(TOKENS, dtype=jnp.int32), mode='drop')
    is_live = owner < TOKENS
    picked = jnp.minimum(owner, TOKENS - 1).astype(jnp.int32)
    zero_val = jnp.zeros((), jnp.bfloat16)
    in_rows = jnp.where(is_live[:, None], normed[picked], zero_val).reshape(E, slot_rows, D)
    cot_rows = jnp.where(is_live[:, None], cotangent[picked], zero_val).reshape(E, slot_rows, D)

    def expert(operands):
        rows_in, rows_cot, up_mat, down_mat = operands
        pre_act = jnp.dot(rows_in, up_mat, preferred_element_type=jnp.float32)
        values, slopes = gelu_parts(pre_act)
        hidden = values.astype(jnp.bfloat16)
        hidden_parts = hidden.astype(jnp.float32).reshape(slot_rows, N_REP, hidden_dev)
        down_parts = down_mat.astype(jnp.float32).reshape(N_REP, hidden_dev, D)
        partial_out = jnp.einsum('srh,rhd->rsd', hidden_parts, down_parts)
        out_rows = lax.optimization_barrier(jnp.sum(partial_out.astype(jnp.bfloat16).astype(jnp.float32), axis=0)).astype(jnp.bfloat16)
        d_act = lax.dot_general(rows_cot, down_mat, (((1,), (1,)), ((), ())), preferred_element_type=jnp.float32)
        d_pre = (d_act * slopes).astype(jnp.bfloat16)
        grad_down = lax.dot_general(hidden, rows_cot, (((0,), (0,)), ((), ())), preferred_element_type=jnp.float32).astype(jnp.bfloat16)
        grad_up = lax.dot_general(rows_in, d_pre, (((0,), (0,)), ((), ())), preferred_element_type=jnp.float32).astype(jnp.bfloat16)
        dpre_parts = d_pre.astype(jnp.float32).reshape(slot_rows, N_REP, hidden_dev)
        up_parts = up_mat.astype(jnp.float32).reshape(D, N_REP, hidden_dev)
        partial_back = jnp.einsum('srh,drh->rsd', dpre_parts, up_parts)
        back_rows = lax.optimization_barrier(jnp.sum(partial_back.astype(jnp.bfloat16).astype(jnp.float32), axis=0)).astype(jnp.bfloat16)
        return (out_rows, back_rows, grad_up, grad_down)
    out_rows, back_rows, grad_up, grad_down = lax.map(expert, (in_rows, cot_rows, up_weight, down_weight))
    token_slot = jnp.minimum(slot_of, E * slot_rows - 1).astype(jnp.int32)
    kept_col = is_kept.reshape(TOKENS, 1)
    mixed = jnp.where(kept_col, out_rows.reshape(E * slot_rows, D)[token_slot], zero_val)
    d_normed = jnp.where(kept_col, back_rows.reshape(E * slot_rows, D)[token_slot], zero_val).astype(jnp.float32)
    gained = d_normed * norm_gain
    cubed = scales * scales * scales
    grad_tokens = (scales * gained - wide_tokens * cubed * lax.optimization_barrier(jnp.mean(gained * wide_tokens, axis=1, keepdims=True))).astype(jnp.bfloat16)
    grad_gain = lax.optimization_barrier(jnp.sum(d_normed * wide_tokens * scales, axis=0))
    return (mixed, grad_tokens, grad_up, grad_down, grad_gain)
```

```python
import functools

import jax
import jax.numpy as jnp
from jax import lax
from jax.experimental import pallas as pl
from jax.experimental.pallas import tpu as pltpu
from jax.sharding import PartitionSpec as P

gelu_coef = 0.7978845608028654
cubic_coef = 0.044715
bf16 = jnp.bfloat16
f32 = jnp.float32
NN = (((1,), (0,)), ((), ()))
NT = (((1,), (1,)), ((), ()))
TN = (((0,), (0,)), ((), ()))


def mm(a, b, dims=NN):
    return lax.dot_general(a, b, dims, preferred_element_type=f32)


def gelu_parts(inputs):
    inner = gelu_coef * (inputs + cubic_coef * inputs * inputs * inputs)
    tangent = jnp.tanh(inner)
    values = 0.5 * inputs * (1.0 + tangent)
    slopes = 0.5 * (1.0 + tangent) + 0.5 * inputs * (1.0 - tangent * tangent) * gelu_coef * (
        1.0 + 3.0 * cubic_coef * inputs * inputs
    )
    return (values, slopes)


def call(kernel, out_shape, args, flops=0, moved=0):
    vmem = pl.BlockSpec(memory_space=pltpu.VMEM)
    return pl.pallas_call(
        kernel,
        out_shape=out_shape,
        in_specs=[vmem] * len(args),
        out_specs=jax.tree.map(lambda _: vmem, out_shape),
        compiler_params=pltpu.CompilerParams(vmem_limit_bytes=48 * 1024 * 1024),
        cost_estimate=pl.CostEstimate(flops=flops, bytes_accessed=moved, transcendentals=0),
    )(*args)


def shaped(shape, dtype=bf16):
    return jax.ShapeDtypeStruct(shape, dtype)


def place_kernel(groups, capacity, tok_ref, id_ref, me_ref, gain_ref, cot_ref, slot_ref, *sends):
    count = tok_ref.shape[0]
    id_row = jnp.broadcast_to(id_ref[...], (count, count))
    id_col = jnp.transpose(id_row)
    at_row = lax.broadcasted_iota(jnp.int32, (count, count), 0)
    at_col = lax.broadcasted_iota(jnp.int32, (count, count), 1)
    earlier = jnp.where((id_row == id_col) & (at_row < at_col), 1, 0)
    ranks = jnp.sum(earlier, axis=0, keepdims=True)
    ahead = id_ref[...] - me_ref[...]
    ahead = jnp.where(ahead < 0, ahead + groups, ahead)
    slots = jnp.where(ranks < capacity, ahead * capacity + ranks, -1)
    slot_ref[...] = slots
    wide = tok_ref[...].astype(f32)
    scales = lax.rsqrt(jnp.mean(wide * wide, axis=1, keepdims=True) + 1e-06)
    normed = (wide * scales * gain_ref[...]).astype(bf16)
    cots = cot_ref[...]
    for k in range(groups):
        rows = lax.broadcasted_iota(jnp.int32, (capacity, count), 0) + k * capacity
        placing = jnp.where(rows == slots, 1.0, 0.0).astype(bf16)
        sends[k][...] = mm(placing, normed).astype(bf16)
        sends[groups + k][...] = mm(placing, cots).astype(bf16)


def forward_kernel(in_ref, up_a, up_b, down_a, down_b, hid_a, hid_b, slope_ref, keep_a, send_a, keep_b, send_b):
    units = up_a.shape[1]
    width = in_ref.shape[1]
    for j, (up, hid) in enumerate(((up_a, hid_a), (up_b, hid_b))):
        step = min(units, 256)

        @pl.loop(0, units // step)
        def _(i):
            at = pl.ds(pl.multiple_of(i * step, step), step)
            values, slopes = gelu_parts(mm(in_ref[...], up[:, at]))
            hid[:, at] = values.astype(bf16)
            slope_ref[j, :, at] = slopes

    quarter = in_ref.shape[0] // 4

    @pl.loop(0, width // 256)
    def _(i):
        at = pl.ds(pl.multiple_of(i * 256, 256), 256)
        total = mm(hid_a[...], down_a[:, at]) + mm(hid_b[...], down_b[:, at])
        keep_a[:, at] = total[:quarter]
        send_a[:, at] = total[quarter : 2 * quarter].astype(bf16)
        keep_b[:, at] = total[2 * quarter : 3 * quarter]
        send_b[:, at] = total[3 * quarter :].astype(bf16)


def backward_kernel(
    cot_ref, in_ref, slope_ref, up_a, up_b, down_a, down_b, pre_a, pre_b, gain_ref, keep_a, send_a, keep_b, send_b
):
    units = up_a.shape[1]
    width = in_ref.shape[1]
    for j, (down, pre) in enumerate(((down_a, pre_a), (down_b, pre_b))):
        step = min(units, 256)

        @pl.loop(0, units // step)
        def _(i):
            at = pl.ds(pl.multiple_of(i * step, step), step)
            pre[:, at] = (mm(cot_ref[...], down[at, :], NT) * slope_ref[j, :, at]).astype(bf16)

    quarter = in_ref.shape[0] // 4

    @pl.loop(0, width // 256)
    def _(i):
        at = pl.ds(pl.multiple_of(i * 256, 256), 256)
        total = mm(pre_a[...], up_a[at, :], NT) + mm(pre_b[...], up_b[at, :], NT)
        gain_ref[:, at] = jnp.sum(total * in_ref[:, at].astype(f32), axis=0, keepdims=True)
        keep_a[:, at] = total[:quarter]
        send_a[:, at] = total[quarter : 2 * quarter].astype(bf16)
        keep_b[:, at] = total[2 * quarter : 3 * quarter]
        send_b[:, at] = total[3 * quarter :].astype(bf16)


def grad_kernel(left_a, left_b, right_a, right_b, out_ref):
    rows = out_ref.shape[0]

    @pl.loop(0, rows // 256)
    def _(i):
        at = pl.ds(pl.multiple_of(i * 256, 256), 256)
        out_ref[at, :] = (mm(left_a[:, at], right_a[...], TN) + mm(left_b[:, at], right_b[...], TN)).astype(bf16)


def mixed_kernel(capacity, slot_ref, *refs):
    out_ref = refs[-1]
    count = slot_ref.shape[1]
    total = None
    for k, ref in enumerate(refs[:-1]):
        rows = lax.broadcasted_iota(jnp.int32, (capacity, count), 0) + k * capacity
        placing = jnp.where(rows == slot_ref[...], 1.0, 0.0).astype(bf16)
        part = mm(placing, ref[...], TN)
        total = part if total is None else total + part
    out_ref[...] = total.astype(bf16)


def token_kernel(capacity, slot_ref, tok_ref, gain_ref, *refs):
    out_ref = refs[-1]
    count = slot_ref.shape[1]
    total = None
    for k, ref in enumerate(refs[:-1]):
        rows = lax.broadcasted_iota(jnp.int32, (capacity, count), 0) + k * capacity
        placing = jnp.where(rows == slot_ref[...], 1.0, 0.0).astype(bf16)
        part = mm(placing, ref[...], TN)
        total = part if total is None else total + part
    wide = tok_ref[...].astype(f32)
    scales = lax.rsqrt(jnp.mean(wide * wide, axis=1, keepdims=True) + 1e-06)
    gained = total * gain_ref[...]
    cubed = scales * scales * scales
    out_ref[...] = (
        scales * gained - wide * (cubed * jnp.mean(gained * wide, axis=1, keepdims=True))
    ).astype(bf16)


def local(tokens, expert_ids, norm_gain, up_weight, down_weight, cotangent):
    groups = lax.axis_size("exp")
    copies = lax.axis_size("rep")
    count, width = tokens.shape
    capacity = 3 * count // (4 * groups)
    slots = groups * capacity
    half = slots // 2
    units = up_weight.shape[2]
    rows = slots * copies // 2
    bits = []
    while (2 << len(bits)) < copies:
        bits.append(2 << len(bits))
    orders = (tuple(bits), tuple(reversed(bits)))

    def swap(x, bit):
        return lax.ppermute(x, "rep", [(i, i ^ bit) for i in range(copies)])

    def shift(x, k):
        return lax.ppermute(x, "exp", [(i, (i + k) % groups) for i in range(groups)])

    up_a, down_a = up_weight[0], down_weight[0]
    up_b, down_b = swap(up_a, 1), swap(down_a, 1)

    me = lax.axis_index("exp").astype(jnp.int32).reshape(1, 1)
    gain_row = norm_gain.reshape(1, width)
    slot_row, *sends = call(
        functools.partial(place_kernel, groups, capacity),
        [shaped((1, count), jnp.int32)] + [shaped((capacity, width))] * (2 * groups),
        (tokens, expert_ids.reshape(1, count), me, gain_row, cotangent),
    )

    def gather(blocks):
        arrived = [blocks[0]] + [shift(blocks[k], k) for k in range(1, groups)]
        halves = [
            jnp.concatenate(arrived[: groups // 2], axis=0),
            jnp.concatenate(arrived[groups // 2 :], axis=0),
        ]
        for i in range(len(bits)):
            for h in range(2):
                halves[h] = jnp.concatenate([halves[h], swap(halves[h], orders[h][i])], axis=0)
        return jnp.concatenate(halves, axis=0)

    def scatter(keeps, sends):
        keeps, sends = list(keeps), list(sends)
        for i in range(len(bits)):
            for h in range(2):
                got = keeps[h] + swap(sends[h], orders[h][len(bits) - 1 - i]).astype(f32)
                cut = got.shape[0] // 2
                if i < len(bits) - 1:
                    keeps[h], sends[h] = got[:cut], got[cut:].astype(bf16)
                else:
                    keeps[h] = got.astype(bf16)
        blocks = []
        for k in range(groups):
            h, at = divmod(k, groups // 2)
            block = keeps[h][at * capacity : (at + 1) * capacity]
            blocks.append(shift(block, groups - k) if k else block)
        return blocks

    in_rows = gather(sends[:groups])
    cot_rows = gather(sends[groups:])
    work = 4 * rows * width * 2 * units
    quarter = rows // 4
    parts = [shaped((quarter, width), f32), shaped((quarter, width))] * 2
    hid_a, hid_b, slopes, *out_parts = call(
        forward_kernel,
        [shaped((rows, units))] * 2 + [shaped((2, rows, units), f32)] + parts,
        (in_rows, up_a, up_b, down_a, down_b),
        work,
        8 << 20,
    )
    pre_a, pre_b, gain_part, *back_parts = call(
        backward_kernel,
        [shaped((rows, units))] * 2 + [shaped((1, width), f32)] + parts,
        (cot_rows, in_rows, slopes, up_a, up_b, down_a, down_b),
        work,
        8 << 20,
    )
    home_out = scatter(out_parts[0::2], out_parts[1::2])
    home_back = scatter(back_parts[0::2], back_parts[1::2])
    grad_down = call(
        grad_kernel,
        shaped((units, width)),
        (hid_a, swap(hid_b, 1), cot_rows, swap(cot_rows, 1)),
        work // 2,
        8 << 20,
    )
    grad_up = call(
        grad_kernel,
        shaped((width, units)),
        (in_rows, swap(in_rows, 1), pre_a, swap(pre_b, 1)),
        work // 2,
        8 << 20,
    )
    total = gain_part
    for bit in [1] + bits:
        total = total + swap(total, bit)
    step = 1
    while step < groups:
        total = total + lax.ppermute(total, "exp", [(i, i ^ step) for i in range(groups)])
        step *= 2
    grad_gain = (total / gain_row).reshape(width)
    mixed = call(functools.partial(mixed_kernel, capacity), shaped((count, width)), (slot_row, *home_out))
    grad_tokens = call(
        functools.partial(token_kernel, capacity), shaped((count, width)), (slot_row, tokens, gain_row, *home_back)
    )
    return (mixed, grad_tokens, grad_up[None], grad_down[None], grad_gain)


def solution(mesh):
    return jax.shard_map(
        local,
        mesh=mesh,
        in_specs=(
            P(("rep", "exp"), None),
            P(("rep", "exp"), None),
            P(),
            P("exp", None, "rep"),
            P("exp", "rep", None),
            P(("rep", "exp"), None),
        ),
        out_specs=(
            P(("rep", "exp"), None),
            P(("rep", "exp"), None),
            P("exp", None, "rep"),
            P("exp", "rep", None),
            P(),
        ),
        check_vma=False,
    )
```

```python
import functools

import jax
import jax.numpy as jnp
from jax import lax
from jax.experimental import pallas as pl
from jax.experimental.pallas import tpu as pltpu
from jax.sharding import PartitionSpec as P

gelu_coef = 0.7978845608028654
cubic_coef = 0.044715
bf16 = jnp.bfloat16
f32 = jnp.float32
NN = (((1,), (0,)), ((), ()))
NT = (((1,), (1,)), ((), ()))
TN = (((0,), (0,)), ((), ()))


ROOM = 20 * 1024 * 1024


def mm(a, b, dims=NN):
    return lax.dot_general(a, b, dims, preferred_element_type=f32)


def gelu_parts(inputs):
    inner = gelu_coef * (inputs + cubic_coef * inputs * inputs * inputs)
    tangent = jnp.tanh(inner)
    values = 0.5 * inputs * (1.0 + tangent)
    slopes = 0.5 * (1.0 + tangent) + 0.5 * inputs * (1.0 - tangent * tangent) * gelu_coef * (
        1.0 + 3.0 * cubic_coef * inputs * inputs
    )
    return (values, slopes)


def call(name, kernel, out_shape, args, flops=0, moved=0, scratch=()):
    vmem = pl.BlockSpec(memory_space=pltpu.VMEM)
    return pl.pallas_call(
        kernel,
        name=name,
        out_shape=out_shape,
        in_specs=[vmem] * len(args),
        out_specs=jax.tree.map(lambda _: vmem, out_shape),
        scratch_shapes=scratch,
        compiler_params=pltpu.CompilerParams(vmem_limit_bytes=ROOM),
        cost_estimate=pl.CostEstimate(flops=flops, bytes_accessed=moved, transcendentals=0),
    )(*args)


def after(values, *events):
    return lax.optimization_barrier((values, events))[0]


def shaped(shape, dtype=bf16):
    return jax.ShapeDtypeStruct(shape, dtype)


def block_places(slot_row, k, capacity):
    at = slot_row - k * capacity
    return jnp.where((at >= 0) & (at < capacity), at, -2 * capacity)


def place_kernel(groups, capacity, tok_ref, id_ref, me_ref, gain_ref, cot_ref, slot_ref, *refs):
    sends, both = refs[:groups], refs[groups]
    count = tok_ref.shape[0]
    id_row = jnp.broadcast_to(id_ref[...], (count, count))
    id_col = jnp.transpose(id_row)
    at_row = lax.broadcasted_iota(jnp.int32, (count, count), 0)
    at_col = lax.broadcasted_iota(jnp.int32, (count, count), 1)
    earlier = jnp.where((id_row == id_col) & (at_row < at_col), 1, 0)
    ranks = jnp.sum(earlier, axis=0, keepdims=True)
    ahead = id_ref[...] - me_ref[...]
    ahead = jnp.where(ahead < 0, ahead + groups, ahead)
    slots = jnp.where(ranks < capacity, ahead * capacity + ranks, -1)
    slot_ref[...] = slots
    wide = tok_ref[...].astype(f32)
    scales = lax.rsqrt(jnp.mean(wide * wide, axis=1, keepdims=True) + 1e-06)
    both[:count] = (wide * scales * gain_ref[...]).astype(bf16)
    both[count:] = cot_ref[...]
    rows = lax.broadcasted_iota(jnp.int32, (2 * capacity, 2 * count), 0)
    for k in range(groups):
        places = block_places(slots, k, capacity)
        wanted = jnp.concatenate([places, places + capacity], axis=1)
        placing = jnp.where(rows == wanted, 1.0, 0.0).astype(bf16)
        sends[k][...] = mm(placing, both[...]).astype(bf16)


def hidden_kernel(in_ref, cot_ref, up_a, up_b, down_a, down_b, hid_a, hid_b, pre_a, pre_b):
    units = up_a.shape[1]
    step = min(units, 256)
    for up, down, hid, pre in ((up_a, down_a, hid_a, pre_a), (up_b, down_b, hid_b, pre_b)):
        for i in range(units // step):
            at = pl.ds(i * step, step)
            values, slopes = gelu_parts(mm(in_ref[...], up[:, at]))
            hid[:, at] = values.astype(bf16)
            pre[:, at] = (mm(cot_ref[...], down[at, :], NT) * slopes).astype(bf16)


def row_kernel(
    piece, in_ref, hid_a, hid_b, pre_a, pre_b, up_a, up_b, down_a, down_b,
    gain_ref, keep_out, send_out, keep_back, send_back,
):
    rows, width = in_ref.shape
    pieces = rows // piece
    for i in range(width // 256):
        at = pl.ds(i * 256, 256)
        total = mm(hid_a[...], down_a[:, at]) + mm(hid_b[...], down_b[:, at])
        keep_out[:, at] = total[: rows // 2]
        send_out[:, at] = total[rows // 2 :].astype(bf16)
        total = mm(pre_a[...], up_a[at, :], NT) + mm(pre_b[...], up_b[at, :], NT)
        gain_ref[:, at] = jnp.sum(total * in_ref[:, at].astype(f32), axis=0, keepdims=True)
        for p in range(pieces):
            part = total[p * piece : (p + 1) * piece]
            to = pl.ds((p // 2) * piece, piece)
            if p % 2:
                send_back[to, at] = part.astype(bf16)
            else:
                keep_back[to, at] = part


def grad_kernel(left_a, left_b, right_a, right_b, out_ref, left, right):
    rows = left_a.shape[0]
    left[:rows], left[rows:] = left_a[...], left_b[...]
    right[:rows], right[rows:] = right_a[...], right_b[...]
    for i in range(out_ref.shape[0] // 256):
        at = pl.ds(i * 256, 256)
        out_ref[at, :] = mm(left[:, at], right[...], TN).astype(bf16)


def token_kernel(capacity, slot_ref, tok_ref, gain_ref, *refs):
    blocks, mixed_ref, grad_ref = refs[:-2], refs[-2], refs[-1]
    count = slot_ref.shape[1]
    rows = lax.broadcasted_iota(jnp.int32, (2 * capacity, count), 0)
    mixed, d_normed = 0.0, 0.0
    for k, ref in enumerate(blocks):
        places = block_places(slot_ref[...], k, capacity)
        block = ref[...]
        mixed += mm(jnp.where(rows == places, 1.0, 0.0).astype(bf16), block, TN)
        d_normed += mm(jnp.where(rows == places + capacity, 1.0, 0.0).astype(bf16), block, TN)
    mixed_ref[...] = mixed.astype(bf16)
    wide = tok_ref[...].astype(f32)
    scales = lax.rsqrt(jnp.mean(wide * wide, axis=1, keepdims=True) + 1e-06)
    gained = d_normed * gain_ref[...]
    cubed = scales * scales * scales
    grad_ref[...] = (
        scales * gained - wide * (cubed * jnp.mean(gained * wide, axis=1, keepdims=True))
    ).astype(bf16)


def local(tokens, expert_ids, norm_gain, up_weight, down_weight, cotangent):
    groups = lax.axis_size("exp")
    copies = lax.axis_size("rep")
    count, width = tokens.shape
    capacity = 3 * count // (4 * groups)
    piece = groups * capacity // 2
    units = up_weight.shape[2]
    rows = piece * copies // 2
    bits = []
    while (2 << len(bits)) < copies:
        bits.append(2 << len(bits))

    def swap(x, bit):
        return lax.ppermute(x, "rep", [(i, i ^ bit) for i in range(copies)])

    def shift(x, k):
        return lax.ppermute(x, "exp", [(i, (i + k) % groups) for i in range(groups)])

    def join(*arrays):
        return jnp.concatenate(arrays, axis=0)

    up_a, down_a = up_weight[0], down_weight[0]
    up_b, down_b = swap(up_a, 1), swap(down_a, 1)

    me = lax.axis_index("exp").astype(jnp.int32).reshape(1, 1)
    gain_row = norm_gain.reshape(1, width)
    slot_row, *blocks = call(
        "place",
        functools.partial(place_kernel, groups, capacity),
        [shaped((1, count), jnp.int32)] + [shaped((2 * capacity, width))] * groups,
        (tokens, expert_ids.reshape(1, count), me, gain_row, cotangent),
        scratch=[pltpu.VMEM((2 * count, width), bf16)],
    )
    arrived = [blocks[0]] + [shift(blocks[k], k) for k in range(1, groups)]

    def start(n, cap_cut):
        mine = range(n * groups // 2, (n + 1) * groups // 2)
        return {0: join(*[arrived[k][cap_cut] for k in mine])}

    def grow(held, bit):
        known = sorted(held)
        got = swap(join(*[held[at] for at in known]), bit)
        return {**held, **{at ^ bit: got[n * piece : (n + 1) * piece] for n, at in enumerate(known)}}

    def ordered(held):
        return join(*[held[at] for at in sorted(held)])

    def halved(x, first):
        cut = x.shape[0] // 2
        if first:
            x = x.reshape(-1, 2, piece, width)
            return x[:, 0].reshape(cut, width), x[:, 1].reshape(cut, width)
        return x[:cut], x[cut:]

    down_bits = list(reversed(bits))
    work = 8 * rows * width * 2 * units
    weights = (up_a, up_b, down_a, down_b)

    def gather(n):
        pair = [start(n, slice(0, capacity)), start(n, slice(capacity, None))]
        for bit, back_bit in zip(bits, down_bits):
            pair = [grow(pair[0], bit), grow(pair[1], back_bit)]
            yield pair

    def compute(in_rows, cot_rows):
        acts = call(
            "hidden",
            hidden_kernel,
            [shaped((rows, units))] * 4,
            (in_rows, cot_rows, *weights),
            work // 2,
            8 << 20,
        )
        kept = [shaped((rows // 2, width), f32), shaped((rows // 2, width))] * 2
        parts = call(
            "rows",
            functools.partial(row_kernel, piece),
            [shaped((1, width), f32)] + kept,
            (in_rows, *acts, *weights),
            work // 2,
            8 << 20,
        )
        return acts, parts

    def scatter(parts, events):
        out, back = parts[1:3], parts[3:5]
        for n, (bit, back_bit) in enumerate(zip(down_bits, bits)):
            got = swap(out[1], bit), swap(back[1], back_bit)
            got = after(got, *events[n])
            out, back = out[0] + got[0].astype(f32), back[0] + got[1].astype(f32)
            if n < len(bits) - 1:
                out, back = halved(out, False), halved(back, True)
                out, back = (out[0], out[1].astype(bf16)), (back[0], back[1].astype(bf16))
                yield (out, back)
            else:
                yield out.astype(bf16), back.astype(bf16)

    def homeward(n, out_rows, back_rows):
        for i in range(groups // 2):
            k = n * groups // 2 + i
            cut = slice(i * capacity, (i + 1) * capacity)
            block = join(out_rows[cut], back_rows[cut])
            home[k] = shift(block, groups - k) if k else block

    *_, first = gather(0)
    steps = list(gather(1))
    in_1, cot_1 = after((ordered(first[0]), ordered(first[1])), steps[-2][0], steps[-2][1])
    acts_1, parts_1 = compute(in_1, cot_1)
    second = after(steps[-1], parts_1[0])
    in_2, cot_2 = ordered(second[0]), ordered(second[1])
    acts_2, parts_2 = compute(in_2, cot_2)
    in_all, cot_all = join(in_1, in_2), join(cot_1, cot_2)
    hid_a, hid_b, pre_a, pre_b = [join(a, b) for a, b in zip(acts_1, acts_2)]
    wide_rows = pltpu.VMEM((4 * rows, width), bf16)
    unit_rows = pltpu.VMEM((4 * rows, units), bf16)
    grad_down = call(
        "grad_down",
        grad_kernel,
        shaped((units, width)),
        (hid_a, swap(hid_b, 1), cot_all, swap(cot_all, 1)),
        work // 4,
        8 << 20,
        [unit_rows, wide_rows],
    )
    grad_up = call(
        "grad_up",
        grad_kernel,
        shaped((width, units)),
        (in_all, swap(in_all, 1), pre_a, swap(pre_b, 1)),
        work // 4,
        8 << 20,
        [wide_rows, unit_rows],
    )
    home = [None] * groups
    *_, sums_1 = scatter(parts_1, [(parts_2[0],)] + [(grad_down,)] * len(bits))
    *_, sums_2 = scatter(parts_2, [(grad_up,)] + [()] * len(bits))
    homeward(0, *sums_1)
    homeward(1, *sums_2)

    total = parts_1[0] + parts_2[0]
    total = after(total, grad_up)
    for bit in [1] + bits:
        total = total + swap(total, bit)
    step = 1
    while step < groups:
        total = total + lax.ppermute(total, "exp", [(i, i ^ step) for i in range(groups)])
        step *= 2
    grad_gain = (total / gain_row).reshape(width)
    mixed, grad_tokens = call(
        "tokens",
        functools.partial(token_kernel, capacity),
        [shaped((count, width))] * 2,
        (slot_row, tokens, gain_row, *home),
    )
    return (mixed, grad_tokens, grad_up[None], grad_down[None], grad_gain)


def solution(mesh):
    return jax.shard_map(
        local,
        mesh=mesh,
        in_specs=(
            P(("rep", "exp"), None),
            P(("rep", "exp"), None),
            P(),
            P("exp", None, "rep"),
            P("exp", "rep", None),
            P(("rep", "exp"), None),
        ),
        out_specs=(
            P(("rep", "exp"), None),
            P(("rep", "exp"), None),
            P("exp", None, "rep"),
            P("exp", "rep", None),
            P(),
        ),
        check_vma=False,
    )
```

```python
import functools

import jax
import jax.numpy as jnp
from jax import lax
from jax.experimental import pallas as pl
from jax.experimental.pallas import tpu as pltpu
from jax.sharding import PartitionSpec as P

gelu_coef = 0.7978845608028654
cubic_coef = 0.044715
bf16 = jnp.bfloat16
f32 = jnp.float32
NN = (((1,), (0,)), ((), ()))
NT = (((1,), (1,)), ((), ()))
TN = (((0,), (0,)), ((), ()))


ROOM = 20 * 1024 * 1024
PLACE_ROOM = 60 * 1024 * 1024


def mm(a, b, dims=NN):
    return lax.dot_general(a, b, dims, preferred_element_type=f32)


def gelu_parts(inputs):
    inner = gelu_coef * (inputs + cubic_coef * inputs * inputs * inputs)
    tangent = jnp.tanh(inner)
    values = 0.5 * inputs * (1.0 + tangent)
    slopes = 0.5 * (1.0 + tangent) + 0.5 * inputs * (1.0 - tangent * tangent) * gelu_coef * (
        1.0 + 3.0 * cubic_coef * inputs * inputs
    )
    return (values, slopes)


def call(name, kernel, out_shape, args, flops=0, moved=0, scratch=(), place=pltpu.VMEM, room=ROOM):
    vmem = pl.BlockSpec(memory_space=pltpu.VMEM)
    return pl.pallas_call(
        kernel,
        name=name,
        out_shape=out_shape,
        in_specs=[pl.BlockSpec(memory_space=place)] * len(args),
        out_specs=jax.tree.map(lambda _: vmem, out_shape),
        scratch_shapes=scratch,
        compiler_params=pltpu.CompilerParams(vmem_limit_bytes=room),
        cost_estimate=pl.CostEstimate(flops=flops, bytes_accessed=moved, transcendentals=0),
    )(*args)


def after(values, *events):
    return lax.optimization_barrier((values, events))[0]


def shaped(shape, dtype=bf16):
    return jax.ShapeDtypeStruct(shape, dtype)


def block_places(slot_row, k, capacity):
    at = slot_row - k * capacity
    return jnp.where((at >= 0) & (at < capacity), at, -2 * capacity)


def place_kernel(groups, capacity, tok_in, id_in, gain_in, cot_in, slot_ref, *refs):
    sends, both, tok_ref, id_ref, gain_ref, sems = refs[:groups], *refs[groups:]
    count = tok_ref.shape[0]
    sources = (id_in, tok_in, gain_in, cot_in)
    targets = (id_ref, tok_ref, gain_ref, both.at[pl.ds(count, count)])
    copies = [pltpu.make_async_copy(a, b, sems.at[i]) for i, (a, b) in enumerate(zip(sources, targets))]
    for copy in copies:
        copy.start()
    copies[0].wait()
    id_row = jnp.broadcast_to(id_ref[...], (count, count))
    id_col = jnp.transpose(id_row)
    at_row = lax.broadcasted_iota(jnp.int32, (count, count), 0)
    at_col = lax.broadcasted_iota(jnp.int32, (count, count), 1)
    earlier = jnp.where((id_row == id_col) & (at_row < at_col), 1, 0)
    ranks = jnp.sum(earlier, axis=0, keepdims=True)
    ahead = id_ref[...] - lax.axis_index("exp").astype(jnp.int32)
    ahead = jnp.where(ahead < 0, ahead + groups, ahead)
    slots = jnp.where(ranks < capacity, ahead * capacity + ranks, -1)
    slot_ref[...] = slots
    copies[1].wait()
    copies[2].wait()
    wide = tok_ref[...].astype(f32)
    scales = lax.rsqrt(jnp.mean(wide * wide, axis=1, keepdims=True) + 1e-06)
    both[:count] = (wide * scales * gain_ref[...]).astype(bf16)
    copies[3].wait()
    rows = lax.broadcasted_iota(jnp.int32, (2 * capacity, 2 * count), 0)
    for k in range(groups):
        places = block_places(slots, k, capacity)
        wanted = jnp.concatenate([places, places + capacity], axis=1)
        placing = jnp.where(rows == wanted, 1.0, 0.0).astype(bf16)
        sends[k][...] = mm(placing, both[...]).astype(bf16)


def hidden_kernel(in_ref, cot_ref, up_a, up_b, down_a, down_b, hid_a, hid_b, pre_a, pre_b):
    units = up_a.shape[1]
    step = min(units, 256)
    for up, down, hid, pre in ((up_a, down_a, hid_a, pre_a), (up_b, down_b, hid_b, pre_b)):
        for i in range(units // step):
            at = pl.ds(i * step, step)
            values, slopes = gelu_parts(mm(in_ref[...], up[:, at]))
            hid[:, at] = values.astype(bf16)
            pre[:, at] = (mm(cot_ref[...], down[at, :], NT) * slopes).astype(bf16)


def row_kernel(
    piece, in_ref, hid_a, hid_b, pre_a, pre_b, up_a, up_b, down_a, down_b,
    gain_ref, keep_out, send_out, keep_back, send_back,
):
    rows, width = in_ref.shape
    pieces = rows // piece
    for i in range(width // 256):
        at = pl.ds(i * 256, 256)
        total = mm(hid_a[...], down_a[:, at]) + mm(hid_b[...], down_b[:, at])
        keep_out[:, at] = total[: rows // 2]
        send_out[:, at] = total[rows // 2 :].astype(bf16)
        total = mm(pre_a[...], up_a[at, :], NT) + mm(pre_b[...], up_b[at, :], NT)
        gain_ref[:, at] = jnp.sum(total * in_ref[:, at].astype(f32), axis=0, keepdims=True)
        for p in range(pieces):
            part = total[p * piece : (p + 1) * piece]
            to = pl.ds((p // 2) * piece, piece)
            if p % 2:
                send_back[to, at] = part.astype(bf16)
            else:
                keep_back[to, at] = part


def grad_kernel(left_a, left_b, right_a, right_b, out_ref, left, right):
    rows = left_a.shape[0]
    left[:rows], left[rows:] = left_a[...], left_b[...]
    right[:rows], right[rows:] = right_a[...], right_b[...]
    for i in range(out_ref.shape[0] // 256):
        at = pl.ds(i * 256, 256)
        out_ref[at, :] = mm(left[:, at], right[...], TN).astype(bf16)


def token_kernel(capacity, slot_ref, tok_ref, gain_ref, *refs):
    blocks, mixed_ref, grad_ref = refs[:-2], refs[-2], refs[-1]
    count = slot_ref.shape[1]
    rows = lax.broadcasted_iota(jnp.int32, (2 * capacity, count), 0)
    mixed, d_normed = 0.0, 0.0
    for k, ref in enumerate(blocks):
        places = block_places(slot_ref[...], k, capacity)
        block = ref[...]
        mixed += mm(jnp.where(rows == places, 1.0, 0.0).astype(bf16), block, TN)
        d_normed += mm(jnp.where(rows == places + capacity, 1.0, 0.0).astype(bf16), block, TN)
    mixed_ref[...] = mixed.astype(bf16)
    wide = tok_ref[...].astype(f32)
    scales = lax.rsqrt(jnp.mean(wide * wide, axis=1, keepdims=True) + 1e-06)
    gained = d_normed * gain_ref[...]
    cubed = scales * scales * scales
    grad_ref[...] = (
        scales * gained - wide * (cubed * jnp.mean(gained * wide, axis=1, keepdims=True))
    ).astype(bf16)


def local(tokens, expert_ids, norm_gain, up_weight, down_weight, cotangent):
    groups = lax.axis_size("exp")
    copies = lax.axis_size("rep")
    count, width = tokens.shape
    capacity = 3 * count // (4 * groups)
    piece = groups * capacity // 2
    units = up_weight.shape[2]
    rows = piece * copies // 2
    bits = []
    while (2 << len(bits)) < copies:
        bits.append(2 << len(bits))

    def swap(x, bit):
        return lax.ppermute(x, "rep", [(i, i ^ bit) for i in range(copies)])

    def shift(x, k):
        return lax.ppermute(x, "exp", [(i, (i + k) % groups) for i in range(groups)])

    def join(*arrays):
        return jnp.concatenate(arrays, axis=0)

    up_a, down_a = up_weight[0], down_weight[0]
    up_b, down_b = swap(up_a, 1), swap(down_a, 1)

    gain_row = norm_gain.reshape(1, width)
    slot_row, *blocks = call(
        "place",
        functools.partial(place_kernel, groups, capacity),
        [shaped((1, count), jnp.int32)] + [shaped((2 * capacity, width))] * groups,
        (tokens, expert_ids.reshape(1, count), gain_row, cotangent),
        scratch=[
            pltpu.VMEM((2 * count, width), bf16),
            pltpu.VMEM((count, width), bf16),
            pltpu.VMEM((1, count), jnp.int32),
            pltpu.VMEM((1, width), f32),
            pltpu.SemaphoreType.DMA((4,)),
        ],
        place=pltpu.HBM,
        room=PLACE_ROOM,
    )
    early = groups // 2
    arrived = [blocks[0]] + [shift(blocks[k], k) for k in range(1, early)]
    blocks = after(blocks, arrived[1:])
    arrived += [shift(blocks[k], k) for k in range(early, groups)]

    def start(n):
        mine = [arrived[k] for k in range(n * groups // 2, (n + 1) * groups // 2)]
        return [{0: join(*[block[:capacity] for block in mine])}, {0: join(*[block[capacity:] for block in mine])}]

    def ordered(held):
        return join(*[held[at] for at in sorted(held)])

    def grow(held, bit):
        known = sorted(held)
        got = swap(ordered(held), bit)
        return {**held, **{at ^ bit: got[n * piece : (n + 1) * piece] for n, at in enumerate(known)}}

    def halved(x, first):
        cut = x.shape[0] // 2
        if first:
            x = x.reshape(-1, 2, piece, width)
            return x[:, 0].reshape(cut, width), x[:, 1].reshape(cut, width)
        return x[:cut], x[cut:]

    down_bits = list(reversed(bits))
    work = 8 * rows * width * 2 * units
    weights = (up_a, up_b, down_a, down_b)

    def gather(pair, events):
        for n, (bit, back_bit) in enumerate(zip(bits, down_bits)):
            pair = after(pair, *events[n]) if n in events else pair
            pair = [grow(pair[0], bit), grow(pair[1], back_bit)]
            yield pair

    def hidden(in_rows, cot_rows):
        return call(
            "hidden",
            hidden_kernel,
            [shaped((rows, units))] * 4,
            (in_rows, cot_rows, *weights),
            work // 2,
            8 << 20,
        )

    def products(in_rows, acts):
        kept = [shaped((rows // 2, width), f32), shaped((rows // 2, width))] * 2
        return call(
            "rows",
            functools.partial(row_kernel, piece),
            [shaped((1, width), f32)] + kept,
            (in_rows, *acts, *weights),
            work // 2,
            8 << 20,
        )

    def packed(sums):
        lead = lax.reduce_precision(sums, 8, 7)
        return jnp.pad(join(lead, sums - lead), ((0, 6), (0, 0))).astype(bf16)

    def unpacked(pair):
        return pair[0:1].astype(f32) + pair[1:2].astype(f32)

    def scatter(parts, events, sums=None):
        out, back = parts[1:3], parts[3:5]
        for n, (bit, back_bit) in enumerate(zip(down_bits, bits)):
            sent = back[1] if sums is None else join(back[1], packed(sums))
            got_out, got_back = after((swap(out[1], bit), swap(sent, back_bit)), *events[n])
            if sums is not None:
                sums = sums + unpacked(got_back[-8:])
                got_back = got_back[:-8]
            out, back = out[0] + got_out.astype(f32), back[0] + got_back.astype(f32)
            if n < len(bits) - 1:
                out, back = halved(out, False), halved(back, True)
                out, back = (out[0], out[1].astype(bf16)), (back[0], back[1].astype(bf16))
        return out.astype(bf16), back.astype(bf16), sums

    def homeward(n, out_rows, back_rows, sums):
        other = []
        for i in range(groups // 2):
            k = n * groups // 2 + i
            cut = slice(i * capacity, (i + 1) * capacity)
            block = join(out_rows[cut], back_rows[cut])
            if k and sums is not None:
                got = shift(join(block, packed(sums)), groups - k)
                other.append(unpacked(got[-8:]))
                home[k] = got[:-8]
            else:
                home[k] = shift(block, groups - k) if k else block
        return other

    steps = list(gather(start(0), {}))
    in_1, cot_1 = [ordered(held) for held in steps[-1]]
    acts_1 = hidden(in_1, cot_1)
    steps = list(gather(start(1), {0: [ordered(held) for held in steps[0]], len(bits) - 1: (acts_1,)}))
    parts_1 = products(after(in_1, steps[-2]), acts_1)
    in_2, cot_2 = [ordered(held) for held in after(steps[-1], parts_1)]
    acts_2 = hidden(in_2, cot_2)
    parts_2 = products(in_2, acts_2)
    in_all, cot_all = join(in_1, in_2), join(cot_1, cot_2)
    hid_a, hid_b, pre_a, pre_b = [join(a, b) for a, b in zip(acts_1, acts_2)]
    wide_rows = pltpu.VMEM((4 * rows, width), bf16)
    unit_rows = pltpu.VMEM((4 * rows, units), bf16)
    grad_down = call(
        "grad_down",
        grad_kernel,
        shaped((units, width)),
        (hid_a, swap(hid_b, 1), cot_all, swap(cot_all, 1)),
        work // 4,
        8 << 20,
        [unit_rows, wide_rows],
    )
    grad_up = call(
        "grad_up",
        grad_kernel,
        shaped((width, units)),
        (in_all, swap(in_all, 1), pre_a, swap(pre_b, 1)),
        work // 4,
        8 << 20,
        [wide_rows, unit_rows],
    )
    home = [None] * groups
    sums = parts_1[0] + parts_2[0]
    sums = sums + swap(sums, 1)
    out_1, back_1, _ = scatter(parts_1, [(parts_2[0],)] + [(grad_down,)] * len(bits))
    out_2, back_2, sums = scatter(parts_2, [(grad_up,)] + [()] * len(bits), sums)
    homeward(0, out_1, back_1, None)
    other = homeward(1, out_2, back_2, sums)
    other += [unpacked(shift(packed(sums), groups - k)) for k in range(1, groups // 2)]
    total = sum(other, sums)
    grad_gain = (total / gain_row).reshape(width)
    mixed, grad_tokens = call(
        "tokens",
        functools.partial(token_kernel, capacity),
        [shaped((count, width))] * 2,
        (slot_row, tokens, gain_row, *home),
    )
    return (mixed, grad_tokens, grad_up[None], grad_down[None], grad_gain)


def solution(mesh):
    return jax.shard_map(
        local,
        mesh=mesh,
        in_specs=(
            P(("rep", "exp"), None),
            P(("rep", "exp"), None),
            P(),
            P("exp", None, "rep"),
            P("exp", "rep", None),
            P(("rep", "exp"), None),
        ),
        out_specs=(
            P(("rep", "exp"), None),
            P(("rep", "exp"), None),
            P("exp", None, "rep"),
            P("exp", "rep", None),
            P(),
        ),
        check_vma=False,
    )
```

```python
import functools

import jax
import jax.numpy as jnp
from jax import lax
from jax.experimental import pallas as pl
from jax.experimental.pallas import tpu as pltpu
from jax.sharding import PartitionSpec as P

gelu_coef = 0.7978845608028654
cubic_coef = 0.044715
bf16 = jnp.bfloat16
f32 = jnp.float32
NN = (((1,), (0,)), ((), ()))
NT = (((1,), (1,)), ((), ()))
TN = (((0,), (0,)), ((), ()))


ROOM = 20 * 1024 * 1024
PLACE_ROOM = 60 * 1024 * 1024


def mm(a, b, dims=NN):
    return lax.dot_general(a, b, dims, preferred_element_type=f32)


def gelu_parts(inputs):
    inner = gelu_coef * (inputs + cubic_coef * inputs * inputs * inputs)
    tangent = jnp.tanh(inner)
    values = 0.5 * inputs * (1.0 + tangent)
    slopes = 0.5 * (1.0 + tangent) + 0.5 * inputs * (1.0 - tangent * tangent) * gelu_coef * (
        1.0 + 3.0 * cubic_coef * inputs * inputs
    )
    return (values, slopes)


def call(name, kernel, out_shape, args, flops=0, moved=0, scratch=(), place=pltpu.VMEM, room=ROOM):
    vmem = pl.BlockSpec(memory_space=pltpu.VMEM)
    return pl.pallas_call(
        kernel,
        name=name,
        out_shape=out_shape,
        in_specs=[pl.BlockSpec(memory_space=place)] * len(args),
        out_specs=jax.tree.map(lambda _: vmem, out_shape),
        scratch_shapes=scratch,
        compiler_params=pltpu.CompilerParams(vmem_limit_bytes=room),
        cost_estimate=pl.CostEstimate(flops=flops, bytes_accessed=moved, transcendentals=0),
    )(*args)


def after(values, *events):
    return lax.optimization_barrier((values, events))[0]


def shaped(shape, dtype=bf16):
    return jax.ShapeDtypeStruct(shape, dtype)


def block_places(slot_row, k, capacity):
    at = slot_row - k * capacity
    return jnp.where((at >= 0) & (at < capacity), at, -2 * capacity)


def place_kernel(groups, capacity, tok_in, id_in, gain_in, cot_in, slot_ref, *refs):
    sends, both, tok_ref, id_ref, gain_ref, sems = refs[:groups], *refs[groups:]
    count = tok_ref.shape[0]
    sources = (id_in, tok_in, gain_in, cot_in)
    targets = (id_ref, tok_ref, gain_ref, both.at[pl.ds(count, count)])
    copies = [pltpu.make_async_copy(a, b, sems.at[i]) for i, (a, b) in enumerate(zip(sources, targets))]
    for copy in copies:
        copy.start()
    copies[0].wait()
    id_row = jnp.broadcast_to(id_ref[...], (count, count))
    id_col = jnp.transpose(id_row)
    at_row = lax.broadcasted_iota(jnp.int32, (count, count), 0)
    at_col = lax.broadcasted_iota(jnp.int32, (count, count), 1)
    earlier = jnp.where((id_row == id_col) & (at_row < at_col), 1, 0)
    ranks = jnp.sum(earlier, axis=0, keepdims=True)
    ahead = id_ref[...] - lax.axis_index("exp").astype(jnp.int32)
    ahead = jnp.where(ahead < 0, ahead + groups, ahead)
    slots = jnp.where(ranks < capacity, ahead * capacity + ranks, -1)
    slot_ref[...] = slots
    copies[1].wait()
    copies[2].wait()
    wide = tok_ref[...].astype(f32)
    scales = lax.rsqrt(jnp.mean(wide * wide, axis=1, keepdims=True) + 1e-06)
    both[:count] = (wide * scales * gain_ref[...]).astype(bf16)
    copies[3].wait()
    rows = lax.broadcasted_iota(jnp.int32, (2 * capacity, 2 * count), 0)
    for k in range(groups):
        places = block_places(slots, k, capacity)
        wanted = jnp.concatenate([places, places + capacity], axis=1)
        placing = jnp.where(rows == wanted, 1.0, 0.0).astype(bf16)
        sends[k][...] = mm(placing, both[...]).astype(bf16)


def hidden_kernel(in_ref, cot_ref, up_a, up_b, down_a, down_b, hid_a, hid_b, pre_a, pre_b):
    units = up_a.shape[1]
    step = min(units, 256)
    for up, down, hid, pre in ((up_a, down_a, hid_a, pre_a), (up_b, down_b, hid_b, pre_b)):
        for i in range(units // step):
            at = pl.ds(i * step, step)
            values, slopes = gelu_parts(mm(in_ref[...], up[:, at]))
            hid[:, at] = values.astype(bf16)
            pre[:, at] = (mm(cot_ref[...], down[at, :], NT) * slopes).astype(bf16)


def row_kernel(
    piece, in_ref, hid_a, hid_b, pre_a, pre_b, up_a, up_b, down_a, down_b,
    gain_ref, keep_out, send_out, keep_back, send_back,
):
    rows, width = in_ref.shape
    pieces = rows // piece
    for i in range(width // 256):
        at = pl.ds(i * 256, 256)
        total = mm(hid_a[...], down_a[:, at]) + mm(hid_b[...], down_b[:, at])
        keep_out[:, at] = total[: rows // 2]
        send_out[:, at] = total[rows // 2 :].astype(bf16)
        total = mm(pre_a[...], up_a[at, :], NT) + mm(pre_b[...], up_b[at, :], NT)
        gain_ref[:, at] = jnp.sum(total * in_ref[:, at].astype(f32), axis=0, keepdims=True)
        for p in range(pieces):
            part = total[p * piece : (p + 1) * piece]
            to = pl.ds((p // 2) * piece, piece)
            if p % 2:
                send_back[to, at] = part.astype(bf16)
            else:
                keep_back[to, at] = part


def grad_kernel(left_a, left_b, right_a, right_b, out_ref, left, right):
    rows = left_a.shape[0]
    left[:rows], left[rows:] = left_a[...], left_b[...]
    right[:rows], right[rows:] = right_a[...], right_b[...]
    for i in range(out_ref.shape[0] // 256):
        at = pl.ds(i * 256, 256)
        out_ref[at, :] = mm(left[:, at], right[...], TN).astype(bf16)


def token_kernel(capacity, slot_ref, tok_ref, gain_ref, *refs):
    blocks, mixed_ref, grad_ref = refs[:-2], refs[-2], refs[-1]
    count = slot_ref.shape[1]
    rows = lax.broadcasted_iota(jnp.int32, (2 * capacity, count), 0)
    mixed, d_normed = 0.0, 0.0
    for k, ref in enumerate(blocks):
        places = block_places(slot_ref[...], k, capacity)
        block = ref[...]
        mixed += mm(jnp.where(rows == places, 1.0, 0.0).astype(bf16), block, TN)
        d_normed += mm(jnp.where(rows == places + capacity, 1.0, 0.0).astype(bf16), block, TN)
    mixed_ref[...] = mixed.astype(bf16)
    wide = tok_ref[...].astype(f32)
    scales = lax.rsqrt(jnp.mean(wide * wide, axis=1, keepdims=True) + 1e-06)
    gained = d_normed * gain_ref[...]
    cubed = scales * scales * scales
    grad_ref[...] = (
        scales * gained - wide * (cubed * jnp.mean(gained * wide, axis=1, keepdims=True))
    ).astype(bf16)


def local(tokens, expert_ids, norm_gain, up_weight, down_weight, cotangent):
    groups = lax.axis_size("exp")
    copies = lax.axis_size("rep")
    count, width = tokens.shape
    capacity = 3 * count // (4 * groups)
    piece = groups * capacity // 2
    units = up_weight.shape[2]
    rows = piece * copies // 2
    bits = []
    while (2 << len(bits)) < copies:
        bits.append(2 << len(bits))

    def swap(x, bit):
        return lax.ppermute(x, "rep", [(i, i ^ bit) for i in range(copies)])

    def shift(x, k):
        return lax.ppermute(x, "exp", [(i, (i + k) % groups) for i in range(groups)])

    def join(*arrays):
        return jnp.concatenate(arrays, axis=0)

    up_a, down_a = up_weight[0], down_weight[0]
    up_b, down_b = swap(up_a, 1), swap(down_a, 1)

    gain_row = norm_gain.reshape(1, width)
    slot_row, *blocks = call(
        "place",
        functools.partial(place_kernel, groups, capacity),
        [shaped((1, count), jnp.int32)] + [shaped((2 * capacity, width))] * groups,
        (tokens, expert_ids.reshape(1, count), gain_row, cotangent),
        scratch=[
            pltpu.VMEM((2 * count, width), bf16),
            pltpu.VMEM((count, width), bf16),
            pltpu.VMEM((1, count), jnp.int32),
            pltpu.VMEM((1, width), f32),
            pltpu.SemaphoreType.DMA((4,)),
        ],
        place=pltpu.HBM,
        room=PLACE_ROOM,
    )
    early = groups // 2
    arrived = [blocks[0]] + [shift(blocks[k], k) for k in range(1, early)]
    blocks = after(blocks, arrived[1:])
    arrived.append(shift(blocks[early], early))

    def start(n):
        mine = [arrived[k] for k in range(n * groups // 2, (n + 1) * groups // 2)]
        return [{0: join(*[block[:capacity] for block in mine])}, {0: join(*[block[capacity:] for block in mine])}]

    def ordered(held):
        return join(*[held[at] for at in sorted(held)])

    def grow(held, bit):
        known = sorted(held)
        got = swap(ordered(held), bit)
        return {**held, **{at ^ bit: got[n * piece : (n + 1) * piece] for n, at in enumerate(known)}}

    def halved(x, first):
        cut = x.shape[0] // 2
        if first:
            x = x.reshape(-1, 2, piece, width)
            return x[:, 0].reshape(cut, width), x[:, 1].reshape(cut, width)
        return x[:cut], x[cut:]

    down_bits = list(reversed(bits))
    work = 8 * rows * width * 2 * units
    weights = (up_a, up_b, down_a, down_b)

    def gather(pair, events):
        for n, (bit, back_bit) in enumerate(zip(bits, down_bits)):
            pair = after(pair, *events[n]) if n in events else pair
            pair = [grow(pair[0], bit), grow(pair[1], back_bit)]
            yield pair

    def hidden(in_rows, cot_rows):
        return call(
            "hidden",
            hidden_kernel,
            [shaped((rows, units))] * 4,
            (in_rows, cot_rows, *weights),
            work // 2,
            8 << 20,
        )

    def products(in_rows, acts):
        kept = [shaped((rows // 2, width), f32), shaped((rows // 2, width))] * 2
        return call(
            "rows",
            functools.partial(row_kernel, piece),
            [shaped((1, width), f32)] + kept,
            (in_rows, *acts, *weights),
            work // 2,
            8 << 20,
        )

    def packed(sums):
        lead = lax.reduce_precision(sums, 8, 7)
        return jnp.pad(join(lead, sums - lead), ((0, 6), (0, 0))).astype(bf16)

    def unpacked(pair):
        return pair[0:1].astype(f32) + pair[1:2].astype(f32)

    def scatter(parts, events, sums=None):
        out, back = parts[1:3], parts[3:5]
        for n, (bit, back_bit) in enumerate(zip(down_bits, bits)):
            sent = back[1] if sums is None else join(back[1], packed(sums))
            got_out, got_back = after((swap(out[1], bit), swap(sent, back_bit)), *events[n])
            if sums is not None:
                sums = sums + unpacked(got_back[-8:])
                got_back = got_back[:-8]
            out, back = out[0] + got_out.astype(f32), back[0] + got_back.astype(f32)
            if n < len(bits) - 1:
                out, back = halved(out, False), halved(back, True)
                out, back = (out[0], out[1].astype(bf16)), (back[0], back[1].astype(bf16))
        return out.astype(bf16), back.astype(bf16), sums

    def homeward(n, out_rows, back_rows, sums):
        other = []
        for i in range(groups // 2):
            k = n * groups // 2 + i
            cut = slice(i * capacity, (i + 1) * capacity)
            block = join(out_rows[cut], back_rows[cut])
            if k and sums is not None:
                got = shift(join(block, packed(sums)), groups - k)
                other.append(unpacked(got[-8:]))
                home[k] = got[:-8]
            else:
                home[k] = shift(block, groups - k) if k else block
        return other

    steps = list(gather(start(0), {}))
    in_1, cot_1 = [ordered(held) for held in steps[-1]]
    acts_1 = hidden(in_1, cot_1)
    events = [ordered(held) for held in steps[0]]
    arrived += [shift(after(blocks[k], events), k) for k in range(early + 1, groups)]
    steps = list(gather(start(1), {0: [ordered(held) for held in steps[0]], len(bits) - 1: (acts_1,)}))
    parts_1 = products(after(in_1, steps[-2]), acts_1)
    in_2, cot_2 = [ordered(held) for held in after(steps[-1], parts_1)]
    acts_2 = hidden(in_2, cot_2)
    parts_2 = products(in_2, acts_2)
    in_all, cot_all = join(in_1, in_2), join(cot_1, cot_2)
    hid_a, hid_b, pre_a, pre_b = [join(a, b) for a, b in zip(acts_1, acts_2)]
    wide_rows = pltpu.VMEM((4 * rows, width), bf16)
    unit_rows = pltpu.VMEM((4 * rows, units), bf16)
    grad_down = call(
        "grad_down",
        grad_kernel,
        shaped((units, width)),
        (hid_a, swap(hid_b, 1), cot_all, swap(cot_all, 1)),
        work // 4,
        8 << 20,
        [unit_rows, wide_rows],
    )
    grad_up = call(
        "grad_up",
        grad_kernel,
        shaped((width, units)),
        (in_all, swap(in_all, 1), pre_a, swap(pre_b, 1)),
        work // 4,
        8 << 20,
        [wide_rows, unit_rows],
    )
    home = [None] * groups
    sums = parts_1[0] + parts_2[0]
    sums = sums + swap(sums, 1)
    out_1, back_1, _ = scatter(parts_1, [(parts_2[0],)] + [(grad_down,)] * len(bits))
    out_2, back_2, sums = scatter(parts_2, [(grad_up,)] + [()] * len(bits), sums)
    homeward(0, out_1, back_1, None)
    other = homeward(1, out_2, back_2, sums)
    other += [unpacked(shift(packed(sums), groups - k)) for k in range(1, groups // 2)]
    total = sum(other, sums)
    grad_gain = (total / gain_row).reshape(width)
    mixed, grad_tokens = call(
        "tokens",
        functools.partial(token_kernel, capacity),
        [shaped((count, width))] * 2,
        (slot_row, tokens, gain_row, *home),
    )
    return (mixed, grad_tokens, grad_up[None], grad_down[None], grad_gain)


def solution(mesh):
    return jax.shard_map(
        local,
        mesh=mesh,
        in_specs=(
            P(("rep", "exp"), None),
            P(("rep", "exp"), None),
            P(),
            P("exp", None, "rep"),
            P("exp", "rep", None),
            P(("rep", "exp"), None),
        ),
        out_specs=(
            P(("rep", "exp"), None),
            P(("rep", "exp"), None),
            P("exp", None, "rep"),
            P("exp", "rep", None),
            P(),
        ),
        check_vma=False,
    )
```

```python
import functools

import jax
import jax.numpy as jnp
from jax import lax
from jax.experimental import pallas as pl
from jax.experimental.pallas import tpu as pltpu
from jax.sharding import PartitionSpec as P

gelu_coef = 0.7978845608028654
cubic_coef = 0.044715
bf16 = jnp.bfloat16
f32 = jnp.float32
NN = (((1,), (0,)), ((), ()))
NT = (((1,), (1,)), ((), ()))
TN = (((0,), (0,)), ((), ()))


ROOM = 20 * 1024 * 1024
PLACE_ROOM = 60 * 1024 * 1024


def mm(a, b, dims=NN):
    return lax.dot_general(a, b, dims, preferred_element_type=f32)


def gelu_parts(inputs):
    inner = gelu_coef * (inputs + cubic_coef * inputs * inputs * inputs)
    tangent = jnp.tanh(inner)
    values = 0.5 * inputs * (1.0 + tangent)
    slopes = 0.5 * (1.0 + tangent) + 0.5 * inputs * (1.0 - tangent * tangent) * gelu_coef * (
        1.0 + 3.0 * cubic_coef * inputs * inputs
    )
    return (values, slopes)


def call(name, kernel, out_shape, args, flops=0, moved=0, scratch=(), place=pltpu.VMEM, room=ROOM):
    vmem = pl.BlockSpec(memory_space=pltpu.VMEM)
    return pl.pallas_call(
        kernel,
        name=name,
        out_shape=out_shape,
        in_specs=[pl.BlockSpec(memory_space=place)] * len(args),
        out_specs=jax.tree.map(lambda _: vmem, out_shape),
        scratch_shapes=scratch,
        compiler_params=pltpu.CompilerParams(vmem_limit_bytes=room),
        cost_estimate=pl.CostEstimate(flops=flops, bytes_accessed=moved, transcendentals=0),
    )(*args)


def after(values, *events):
    return lax.optimization_barrier((values, events))[0]


def shaped(shape, dtype=bf16):
    return jax.ShapeDtypeStruct(shape, dtype)


def block_places(slot_row, k, capacity):
    at = slot_row - k * capacity
    return jnp.where((at >= 0) & (at < capacity), at, -2 * capacity)


def place_kernel(groups, capacity, tok_in, id_in, gain_in, cot_in, slot_ref, *refs):
    sends, both, tok_ref, id_ref, gain_ref, sems = refs[:groups], *refs[groups:]
    count = tok_ref.shape[0]
    sources = (id_in, tok_in, gain_in, cot_in)
    targets = (id_ref, tok_ref, gain_ref, both.at[pl.ds(count, count)])
    copies = [pltpu.make_async_copy(a, b, sems.at[i]) for i, (a, b) in enumerate(zip(sources, targets))]
    for copy in copies:
        copy.start()
    copies[0].wait()
    id_row = jnp.broadcast_to(id_ref[...], (count, count))
    id_col = jnp.transpose(id_row)
    at_row = lax.broadcasted_iota(jnp.int32, (count, count), 0)
    at_col = lax.broadcasted_iota(jnp.int32, (count, count), 1)
    earlier = jnp.where((id_row == id_col) & (at_row < at_col), 1, 0)
    ranks = jnp.sum(earlier, axis=0, keepdims=True)
    ahead = id_ref[...] - lax.axis_index("exp").astype(jnp.int32)
    ahead = jnp.where(ahead < 0, ahead + groups, ahead)
    slots = jnp.where(ranks < capacity, ahead * capacity + ranks, -1)
    slot_ref[...] = slots
    copies[1].wait()
    copies[2].wait()
    wide = tok_ref[...].astype(f32)
    scales = lax.rsqrt(jnp.mean(wide * wide, axis=1, keepdims=True) + 1e-06)
    both[:count] = (wide * scales * gain_ref[...]).astype(bf16)
    copies[3].wait()
    rows = lax.broadcasted_iota(jnp.int32, (2 * capacity, 2 * count), 0)
    for k in range(groups):
        places = block_places(slots, k, capacity)
        wanted = jnp.concatenate([places, places + capacity], axis=1)
        placing = jnp.where(rows == wanted, 1.0, 0.0).astype(bf16)
        sends[k][...] = mm(placing, both[...]).astype(bf16)


def pack_kernel(up_ref, down_ref, pack_ref):
    units = up_ref.shape[1]
    pack_ref[:, :units] = up_ref[...]
    for j in range(up_ref.shape[0] // units):
        at = pl.ds(j * units, units)
        pack_ref[at, units:] = down_ref[:, at]


def hidden_kernel(in_ref, cot_ref, up_a, down_a, pack_b, hid_a, hid_b, pre_a, pre_b):
    width, units = up_a.shape
    step = min(units, 256)
    for i in range(units // step):
        at = pl.ds(i * step, step)
        values, slopes = gelu_parts(mm(in_ref[...], up_a[:, at]))
        hid_a[:, at] = values.astype(bf16)
        pre_a[:, at] = (mm(cot_ref[...], down_a[at, :], NT) * slopes).astype(bf16)
    for i in range(units // step):
        at = pl.ds(i * step, step)
        values, slopes = gelu_parts(mm(in_ref[...], pack_b[:, at]))
        hid_b[:, at] = values.astype(bf16)
        total = None
        for j in range(width // units):
            block = pack_b[pl.ds(j * units + i * step, step), pl.ds(units, units)]
            part = mm(cot_ref[:, pl.ds(j * units, units)], block, NT)
            total = part if total is None else total + part
        pre_b[:, at] = (total * slopes).astype(bf16)


def row_kernel(
    piece, in_ref, hid_a, hid_b, pre_a, pre_b, up_a, down_a, pack_b,
    gain_ref, keep_out, send_out, keep_back, send_back,
):
    rows, width = in_ref.shape
    pieces = rows // piece
    units = up_a.shape[1]
    for i in range(width // 256):
        at = pl.ds(i * 256, 256)
        j, off = divmod(i * 256, units)
        down_b = pack_b[pl.ds(j * units, units), pl.ds(units + off, 256)]
        total = mm(hid_a[...], down_a[:, at]) + mm(hid_b[...], down_b)
        keep_out[:, at] = total[: rows // 2]
        send_out[:, at] = total[rows // 2 :].astype(bf16)
        total = mm(pre_a[...], up_a[at, :], NT) + mm(pre_b[...], pack_b[at, pl.ds(0, units)], NT)
        gain_ref[:, at] = jnp.sum(total * in_ref[:, at].astype(f32), axis=0, keepdims=True)
        for p in range(pieces):
            part = total[p * piece : (p + 1) * piece]
            to = pl.ds((p // 2) * piece, piece)
            if p % 2:
                send_back[to, at] = part.astype(bf16)
            else:
                keep_back[to, at] = part


def grad_kernel(left_a, left_b, right_a, right_b, out_ref, left, right):
    rows = left_a.shape[0]
    left[:rows], left[rows:] = left_a[...], left_b[...]
    right[:rows], right[rows:] = right_a[...], right_b[...]
    for i in range(out_ref.shape[0] // 256):
        at = pl.ds(i * 256, 256)
        out_ref[at, :] = mm(left[:, at], right[...], TN).astype(bf16)


def token_kernel(capacity, slot_ref, tok_ref, gain_ref, *refs):
    blocks, mixed_ref, grad_ref = refs[:-2], refs[-2], refs[-1]
    count = slot_ref.shape[1]
    rows = lax.broadcasted_iota(jnp.int32, (2 * capacity, count), 0)
    mixed, d_normed = 0.0, 0.0
    for k, ref in enumerate(blocks):
        places = block_places(slot_ref[...], k, capacity)
        block = ref[...]
        mixed += mm(jnp.where(rows == places, 1.0, 0.0).astype(bf16), block, TN)
        d_normed += mm(jnp.where(rows == places + capacity, 1.0, 0.0).astype(bf16), block, TN)
    mixed_ref[...] = mixed.astype(bf16)
    wide = tok_ref[...].astype(f32)
    scales = lax.rsqrt(jnp.mean(wide * wide, axis=1, keepdims=True) + 1e-06)
    gained = d_normed * gain_ref[...]
    cubed = scales * scales * scales
    grad_ref[...] = (
        scales * gained - wide * (cubed * jnp.mean(gained * wide, axis=1, keepdims=True))
    ).astype(bf16)


def local(tokens, expert_ids, norm_gain, up_weight, down_weight, cotangent):
    groups = lax.axis_size("exp")
    copies = lax.axis_size("rep")
    count, width = tokens.shape
    capacity = 3 * count // (4 * groups)
    piece = groups * capacity // 2
    units = up_weight.shape[2]
    rows = piece * copies // 2
    bits = []
    while (2 << len(bits)) < copies:
        bits.append(2 << len(bits))

    def swap(x, bit):
        return lax.ppermute(x, "rep", [(i, i ^ bit) for i in range(copies)])

    def shift(x, k):
        return lax.ppermute(x, "exp", [(i, (i + k) % groups) for i in range(groups)])

    def join(*arrays):
        return jnp.concatenate(arrays, axis=0)

    up_a, down_a = up_weight[0], down_weight[0]

    gain_row = norm_gain.reshape(1, width)
    slot_row, *blocks = call(
        "place",
        functools.partial(place_kernel, groups, capacity),
        [shaped((1, count), jnp.int32)] + [shaped((2 * capacity, width))] * groups,
        (tokens, expert_ids.reshape(1, count), gain_row, cotangent),
        scratch=[
            pltpu.VMEM((2 * count, width), bf16),
            pltpu.VMEM((count, width), bf16),
            pltpu.VMEM((1, count), jnp.int32),
            pltpu.VMEM((1, width), f32),
            pltpu.SemaphoreType.DMA((4,)),
        ],
        place=pltpu.HBM,
        room=PLACE_ROOM,
    )
    pack_a = call(
        "pack",
        pack_kernel,
        shaped((width, 2 * units)),
        after((up_a, down_a), blocks[0]),
        2,
        8 << 20,
    )
    pack_b = swap(pack_a, 1)
    early = groups // 2
    arrived = [blocks[0]] + [shift(blocks[k], k) for k in range(1, early)]
    blocks = after(blocks, arrived[1:])
    arrived.append(shift(blocks[early], early))

    def start(n):
        mine = [arrived[k] for k in range(n * groups // 2, (n + 1) * groups // 2)]
        return [{0: join(*[block[:capacity] for block in mine])}, {0: join(*[block[capacity:] for block in mine])}]

    def ordered(held):
        return join(*[held[at] for at in sorted(held)])

    def grow(held, bit):
        known = sorted(held)
        got = swap(ordered(held), bit)
        return {**held, **{at ^ bit: got[n * piece : (n + 1) * piece] for n, at in enumerate(known)}}

    def halved(x, first):
        cut = x.shape[0] // 2
        if first:
            x = x.reshape(-1, 2, piece, width)
            return x[:, 0].reshape(cut, width), x[:, 1].reshape(cut, width)
        return x[:cut], x[cut:]

    down_bits = list(reversed(bits))
    work = 8 * rows * width * 2 * units
    weights = (up_a, down_a, pack_b)

    def gather(pair, events):
        for n, (bit, back_bit) in enumerate(zip(bits, down_bits)):
            pair = after(pair, *events[n]) if n in events else pair
            pair = [grow(pair[0], bit), grow(pair[1], back_bit)]
            yield pair

    def hidden(in_rows, cot_rows):
        return call(
            "hidden",
            hidden_kernel,
            [shaped((rows, units))] * 4,
            (in_rows, cot_rows, *weights),
            work // 2,
            8 << 20,
        )

    def products(in_rows, acts):
        kept = [shaped((rows // 2, width), f32), shaped((rows // 2, width))] * 2
        return call(
            "rows",
            functools.partial(row_kernel, piece),
            [shaped((1, width), f32)] + kept,
            (in_rows, *acts, *weights),
            work // 2,
            8 << 20,
        )

    def packed(sums):
        lead = lax.reduce_precision(sums, 8, 7)
        return jnp.pad(join(lead, sums - lead), ((0, 6), (0, 0))).astype(bf16)

    def unpacked(pair):
        return pair[0:1].astype(f32) + pair[1:2].astype(f32)

    def scatter(parts, events, sums=None):
        out, back = parts[1:3], parts[3:5]
        for n, (bit, back_bit) in enumerate(zip(down_bits, bits)):
            sent = back[1] if sums is None else join(back[1], packed(sums))
            got_out, got_back = after((swap(out[1], bit), swap(sent, back_bit)), *events[n])
            if sums is not None:
                sums = sums + unpacked(got_back[-8:])
                got_back = got_back[:-8]
            out, back = out[0] + got_out.astype(f32), back[0] + got_back.astype(f32)
            if n < len(bits) - 1:
                out, back = halved(out, False), halved(back, True)
                out, back = (out[0], out[1].astype(bf16)), (back[0], back[1].astype(bf16))
        return out.astype(bf16), back.astype(bf16), sums

    def homeward(n, out_rows, back_rows, sums):
        other = []
        for i in range(groups // 2):
            k = n * groups // 2 + i
            cut = slice(i * capacity, (i + 1) * capacity)
            block = join(out_rows[cut], back_rows[cut])
            if k and sums is not None:
                home[k] = shift(block, groups - k)
            else:
                home[k] = shift(block, groups - k) if k else block
        return other

    steps = list(gather(start(0), {}))
    in_1, cot_1 = [ordered(held) for held in steps[-1]]
    acts_1 = hidden(in_1, cot_1)
    events = [ordered(held) for held in steps[0]]
    arrived += [shift(after(blocks[k], events), k) for k in range(early + 1, groups)]
    steps = list(gather(start(1), {0: [ordered(held) for held in steps[0]], len(bits) - 1: (acts_1,)}))
    parts_1 = products(after(in_1, steps[-2]), acts_1)
    in_2, cot_2 = [ordered(held) for held in after(steps[-1], parts_1)]
    acts_2 = hidden(in_2, cot_2)
    parts_2 = products(in_2, acts_2)
    in_all, cot_all = join(in_1, in_2), join(cot_1, cot_2)
    hid_a, hid_b, pre_a, pre_b = [join(a, b) for a, b in zip(acts_1, acts_2)]
    wide_rows = pltpu.VMEM((4 * rows, width), bf16)
    unit_rows = pltpu.VMEM((4 * rows, units), bf16)
    grad_down = call(
        "grad_down",
        grad_kernel,
        shaped((units, width)),
        (hid_a, swap(hid_b, 1), cot_all, swap(cot_all, 1)),
        work // 4,
        8 << 20,
        [unit_rows, wide_rows],
    )
    grad_up = call(
        "grad_up",
        grad_kernel,
        shaped((width, units)),
        (in_all, swap(in_all, 1), pre_a, swap(pre_b, 1)),
        work // 4,
        8 << 20,
        [wide_rows, unit_rows],
    )
    home = [None] * groups
    sums = parts_1[0] + parts_2[0]
    sums = sums + swap(sums, 1)
    out_1, back_1, _ = scatter(parts_1, [(sums,)] + [(grad_down,)] * len(bits))
    out_2, back_2, sums = scatter(parts_2, [(grad_up,)] + [()] * len(bits), sums)
    homeward(0, out_1, back_1, None)
    other = homeward(1, out_2, back_2, sums)
    total = sums.reshape(16, width // 16)
    step = 1
    while step < groups:
        total = total + lax.ppermute(total, "exp", [(i, i ^ step) for i in range(groups)])
        step *= 2
    total = total.reshape(1, width)
    grad_gain = (total / gain_row).reshape(width)
    mixed, grad_tokens = call(
        "tokens",
        functools.partial(token_kernel, capacity),
        [shaped((count, width))] * 2,
        (slot_row, tokens, gain_row, *home),
    )
    return (mixed, grad_tokens, grad_up[None], grad_down[None], grad_gain)


def solution(mesh):
    return jax.shard_map(
        local,
        mesh=mesh,
        in_specs=(
            P(("rep", "exp"), None),
            P(("rep", "exp"), None),
            P(),
            P("exp", None, "rep"),
            P("exp", "rep", None),
            P(("rep", "exp"), None),
        ),
        out_specs=(
            P(("rep", "exp"), None),
            P(("rep", "exp"), None),
            P("exp", None, "rep"),
            P("exp", "rep", None),
            P(),
        ),
        check_vma=False,
    )
```

```python
import functools

import jax
import jax.numpy as jnp
from jax import lax
from jax.experimental import pallas as pl
from jax.experimental.pallas import tpu as pltpu
from jax.sharding import PartitionSpec as P

gelu_coef = 0.7978845608028654
cubic_coef = 0.044715
bf16 = jnp.bfloat16
f32 = jnp.float32
NN = (((1,), (0,)), ((), ()))
NT = (((1,), (1,)), ((), ()))
TN = (((0,), (0,)), ((), ()))


ROOM = 20 * 1024 * 1024
PLACE_ROOM = 60 * 1024 * 1024


def mm(a, b, dims=NN):
    return lax.dot_general(a, b, dims, preferred_element_type=f32)


def gelu_parts(inputs):
    inner = gelu_coef * (inputs + cubic_coef * inputs * inputs * inputs)
    tangent = jnp.tanh(inner)
    values = 0.5 * inputs * (1.0 + tangent)
    slopes = 0.5 * (1.0 + tangent) + 0.5 * inputs * (1.0 - tangent * tangent) * gelu_coef * (
        1.0 + 3.0 * cubic_coef * inputs * inputs
    )
    return (values, slopes)


def call(name, kernel, out_shape, args, flops=0, moved=0, scratch=(), place=pltpu.VMEM, room=ROOM):
    vmem = pl.BlockSpec(memory_space=pltpu.VMEM)
    return pl.pallas_call(
        kernel,
        name=name,
        out_shape=out_shape,
        in_specs=[pl.BlockSpec(memory_space=place)] * len(args),
        out_specs=jax.tree.map(lambda _: vmem, out_shape),
        scratch_shapes=scratch,
        compiler_params=pltpu.CompilerParams(vmem_limit_bytes=room),
        cost_estimate=pl.CostEstimate(flops=flops, bytes_accessed=moved, transcendentals=0),
    )(*args)


def after(values, *events):
    return lax.optimization_barrier((values, events))[0]


def shaped(shape, dtype=bf16):
    return jax.ShapeDtypeStruct(shape, dtype)


def block_places(slot_row, k, capacity):
    at = slot_row - k * capacity
    return jnp.where((at >= 0) & (at < capacity), at, -2 * capacity)


def place_kernel(groups, capacity, tok_in, id_in, gain_in, cot_in, slot_ref, *refs):
    sends, both, tok_ref, id_ref, gain_ref, sems = refs[:groups], *refs[groups:]
    count = tok_ref.shape[0]
    sources = (id_in, tok_in, gain_in, cot_in)
    targets = (id_ref, tok_ref, gain_ref, both.at[pl.ds(count, count)])
    copies = [pltpu.make_async_copy(a, b, sems.at[i]) for i, (a, b) in enumerate(zip(sources, targets))]
    for copy in copies:
        copy.start()
    copies[0].wait()
    id_row = jnp.broadcast_to(id_ref[...], (count, count))
    id_col = jnp.transpose(id_row)
    at_row = lax.broadcasted_iota(jnp.int32, (count, count), 0)
    at_col = lax.broadcasted_iota(jnp.int32, (count, count), 1)
    earlier = jnp.where((id_row == id_col) & (at_row < at_col), 1, 0)
    ranks = jnp.sum(earlier, axis=0, keepdims=True)
    ahead = id_ref[...] - lax.axis_index("exp").astype(jnp.int32)
    ahead = jnp.where(ahead < 0, ahead + groups, ahead)
    slots = jnp.where(ranks < capacity, ahead * capacity + ranks, -1)
    slot_ref[...] = jnp.where(slots < 0, -2 * groups * capacity, ahead * 2 * capacity + ranks)
    copies[1].wait()
    copies[2].wait()
    wide = tok_ref[...].astype(f32)
    scales = lax.rsqrt(jnp.mean(wide * wide, axis=1, keepdims=True) + 1e-06)
    both[:count] = (wide * scales * gain_ref[...]).astype(bf16)
    copies[3].wait()
    rows = lax.broadcasted_iota(jnp.int32, (2 * capacity, 2 * count), 0)
    for k in range(groups):
        places = block_places(slots, k, capacity)
        wanted = jnp.concatenate([places, places + capacity], axis=1)
        placing = jnp.where(rows == wanted, 1.0, 0.0).astype(bf16)
        sends[k][...] = mm(placing, both[...]).astype(bf16)


def pack_kernel(up_ref, down_ref, pack_ref):
    units = up_ref.shape[1]
    pack_ref[:, :units] = up_ref[...]
    for j in range(up_ref.shape[0] // units):
        at = pl.ds(j * units, units)
        pack_ref[at, units:] = down_ref[:, at]


def hidden_kernel(in_ref, cot_ref, up_a, down_a, pack_b, hid_a, hid_b, pre_a, pre_b):
    width, units = up_a.shape
    step = min(units, 256)
    for i in range(units // step):
        at = pl.ds(i * step, step)
        values, slopes = gelu_parts(mm(in_ref[...], up_a[:, at]))
        hid_a[:, at] = values.astype(bf16)
        pre_a[:, at] = (mm(cot_ref[...], down_a[at, :], NT) * slopes).astype(bf16)
    for i in range(units // step):
        at = pl.ds(i * step, step)
        values, slopes = gelu_parts(mm(in_ref[...], pack_b[:, at]))
        hid_b[:, at] = values.astype(bf16)
        total = None
        for j in range(width // units):
            block = pack_b[pl.ds(j * units + i * step, step), pl.ds(units, units)]
            part = mm(cot_ref[:, pl.ds(j * units, units)], block, NT)
            total = part if total is None else total + part
        pre_b[:, at] = (total * slopes).astype(bf16)


def row_kernel(
    piece, in_ref, hid_a, hid_b, pre_a, pre_b, up_a, down_a, pack_b,
    gain_ref, keep_out, send_out, keep_back, send_back,
):
    rows, width = in_ref.shape
    pieces = rows // piece
    units = up_a.shape[1]
    for i in range(width // 256):
        at = pl.ds(i * 256, 256)
        j, off = divmod(i * 256, units)
        down_b = pack_b[pl.ds(j * units, units), pl.ds(units + off, 256)]
        total = mm(hid_a[...], down_a[:, at]) + mm(hid_b[...], down_b)
        keep_out[:, at] = total[: rows // 2]
        send_out[:, at] = total[rows // 2 :].astype(bf16)
        total = mm(pre_a[...], up_a[at, :], NT) + mm(pre_b[...], pack_b[at, pl.ds(0, units)], NT)
        gain_ref[:, at] = jnp.sum(total * in_ref[:, at].astype(f32), axis=0, keepdims=True)
        for p in range(pieces):
            part = total[p * piece : (p + 1) * piece]
            to = pl.ds((p // 2) * piece, piece)
            if p % 2:
                send_back[to, at] = part.astype(bf16)
            else:
                keep_back[to, at] = part


def grad_kernel(left_a, left_b, right_a, right_b, out_ref, left, right):
    rows = left_a.shape[0]
    left[:rows], left[rows:] = left_a[...], left_b[...]
    right[:rows], right[rows:] = right_a[...], right_b[...]
    for i in range(out_ref.shape[0] // 256):
        at = pl.ds(i * 256, 256)
        out_ref[at, :] = mm(left[:, at], right[...], TN).astype(bf16)


def token_kernel(capacity, slot_ref, tok_ref, gain_ref, *refs):
    blocks, mixed_ref, grad_ref = refs[:-2], refs[-2], refs[-1]
    count = slot_ref.shape[1]
    wanted = jnp.concatenate([slot_ref[...], slot_ref[...] + capacity], axis=1)
    if 2 * capacity % 16:
        parts = [ref[...] for ref in blocks]
    else:
        parts = [jnp.concatenate([ref[...] for ref in blocks], axis=0)]
    found, start = 0.0, 0
    for part in parts:
        rows = lax.broadcasted_iota(jnp.int32, (part.shape[0], 2 * count), 0) + start
        found += mm(jnp.where(rows == wanted, 1.0, 0.0).astype(bf16), part, TN)
        start += part.shape[0]
    mixed, d_normed = found[:count], found[count:]
    mixed_ref[...] = mixed.astype(bf16)
    wide = tok_ref[...].astype(f32)
    scales = lax.rsqrt(jnp.mean(wide * wide, axis=1, keepdims=True) + 1e-06)
    gained = d_normed * gain_ref[...]
    cubed = scales * scales * scales
    grad_ref[...] = (
        scales * gained - wide * (cubed * jnp.mean(gained * wide, axis=1, keepdims=True))
    ).astype(bf16)


def local(tokens, expert_ids, norm_gain, up_weight, down_weight, cotangent):
    groups = lax.axis_size("exp")
    copies = lax.axis_size("rep")
    count, width = tokens.shape
    capacity = 3 * count // (4 * groups)
    piece = groups * capacity // 2
    units = up_weight.shape[2]
    rows = piece * copies // 2
    bits = []
    while (2 << len(bits)) < copies:
        bits.append(2 << len(bits))

    def swap(x, bit):
        return lax.ppermute(x, "rep", [(i, i ^ bit) for i in range(copies)])

    def shift(x, k):
        return lax.ppermute(x, "exp", [(i, (i + k) % groups) for i in range(groups)])

    def join(*arrays):
        return jnp.concatenate(arrays, axis=0)

    up_a, down_a = up_weight[0], down_weight[0]

    gain_row = norm_gain.reshape(1, width)
    slot_row, *blocks = call(
        "place",
        functools.partial(place_kernel, groups, capacity),
        [shaped((1, count), jnp.int32)] + [shaped((2 * capacity, width))] * groups,
        (tokens, expert_ids.reshape(1, count), gain_row, cotangent),
        scratch=[
            pltpu.VMEM((2 * count, width), bf16),
            pltpu.VMEM((count, width), bf16),
            pltpu.VMEM((1, count), jnp.int32),
            pltpu.VMEM((1, width), f32),
            pltpu.SemaphoreType.DMA((4,)),
        ],
        place=pltpu.HBM,
        room=PLACE_ROOM,
    )
    pack_a = call(
        "pack",
        pack_kernel,
        shaped((width, 2 * units)),
        after((up_a, down_a), blocks[0]),
        2,
        8 << 20,
    )
    pack_b = swap(pack_a, 1)
    early = groups // 2
    arrived = [blocks[0]] + [shift(blocks[k], k) for k in range(1, early)]
    blocks = after(blocks, arrived[1:])
    arrived.append(shift(blocks[early], early))

    def start(n):
        mine = [arrived[k] for k in range(n * groups // 2, (n + 1) * groups // 2)]
        return [{0: join(*[block[:capacity] for block in mine])}, {0: join(*[block[capacity:] for block in mine])}]

    def ordered(held):
        return join(*[held[at] for at in sorted(held)])

    def grow(held, bit):
        known = sorted(held)
        got = swap(ordered(held), bit)
        return {**held, **{at ^ bit: got[n * piece : (n + 1) * piece] for n, at in enumerate(known)}}

    def halved(x, first):
        cut = x.shape[0] // 2
        if first:
            x = x.reshape(-1, 2, piece, width)
            return x[:, 0].reshape(cut, width), x[:, 1].reshape(cut, width)
        return x[:cut], x[cut:]

    down_bits = list(reversed(bits))
    work = 8 * rows * width * 2 * units
    weights = (up_a, down_a, pack_b)

    def gather(pair, events):
        for n, (bit, back_bit) in enumerate(zip(bits, down_bits)):
            pair = after(pair, *events[n]) if n in events else pair
            pair = [grow(pair[0], bit), grow(pair[1], back_bit)]
            yield pair

    def hidden(in_rows, cot_rows):
        return call(
            "hidden",
            hidden_kernel,
            [shaped((rows, units))] * 4,
            (in_rows, cot_rows, *weights),
            work // 2,
            8 << 20,
        )

    def products(in_rows, acts):
        kept = [shaped((rows // 2, width), f32), shaped((rows // 2, width))] * 2
        return call(
            "rows",
            functools.partial(row_kernel, piece),
            [shaped((1, width), f32)] + kept,
            (in_rows, *acts, *weights),
            work // 2,
            8 << 20,
        )

    def packed(sums):
        lead = lax.reduce_precision(sums, 8, 7)
        return jnp.pad(join(lead, sums - lead), ((0, 6), (0, 0))).astype(bf16)

    def unpacked(pair):
        return pair[0:1].astype(f32) + pair[1:2].astype(f32)

    def scatter(parts, events, sums=None):
        out, back = parts[1:3], parts[3:5]
        for n, (bit, back_bit) in enumerate(zip(down_bits, bits)):
            sent = back[1] if sums is None else join(back[1], packed(sums))
            got_out, got_back = after((swap(out[1], bit), swap(sent, back_bit)), *events[n])
            if sums is not None:
                sums = sums + unpacked(got_back[-8:])
                got_back = got_back[:-8]
            out, back = out[0] + got_out.astype(f32), back[0] + got_back.astype(f32)
            if n < len(bits) - 1:
                out, back = halved(out, False), halved(back, True)
                out, back = (out[0], out[1].astype(bf16)), (back[0], back[1].astype(bf16))
        return out.astype(bf16), back.astype(bf16), sums

    def homeward(n, out_rows, back_rows, sums):
        other = []
        for i in range(groups // 2):
            k = n * groups // 2 + i
            cut = slice(i * capacity, (i + 1) * capacity)
            block = join(out_rows[cut], back_rows[cut])
            if k and sums is not None:
                home[k] = shift(block, groups - k)
            else:
                home[k] = shift(block, groups - k) if k else block
        return other

    steps = list(gather(start(0), {}))
    in_1, cot_1 = [ordered(held) for held in steps[-1]]
    acts_1 = hidden(in_1, cot_1)
    events = [ordered(held) for held in steps[0]]
    arrived += [shift(after(blocks[k], events), k) for k in range(early + 1, groups)]
    steps = list(gather(start(1), {0: [ordered(held) for held in steps[0]], len(bits) - 1: (acts_1,)}))
    parts_1 = products(after(in_1, steps[-2]), acts_1)
    in_2, cot_2 = [ordered(held) for held in after(steps[-1], parts_1)]
    acts_2 = hidden(in_2, cot_2)
    parts_2 = products(in_2, acts_2)
    in_all, cot_all = join(in_1, in_2), join(cot_1, cot_2)
    hid_a, hid_b, pre_a, pre_b = [join(a, b) for a, b in zip(acts_1, acts_2)]
    wide_rows = pltpu.VMEM((4 * rows, width), bf16)
    unit_rows = pltpu.VMEM((4 * rows, units), bf16)
    grad_down = call(
        "grad_down",
        grad_kernel,
        shaped((units, width)),
        (hid_a, swap(hid_b, 1), cot_all, swap(cot_all, 1)),
        work // 4,
        8 << 20,
        [unit_rows, wide_rows],
    )
    grad_up = call(
        "grad_up",
        grad_kernel,
        shaped((width, units)),
        (in_all, swap(in_all, 1), pre_a, swap(pre_b, 1)),
        work // 4,
        8 << 20,
        [wide_rows, unit_rows],
    )
    home = [None] * groups
    sums = parts_1[0] + parts_2[0]
    sums = sums + swap(sums, 1)
    out_1, back_1, _ = scatter(parts_1, [(sums,)] + [(grad_down,)] * len(bits))
    out_2, back_2, sums = scatter(parts_2, [(grad_up,)] + [()] * len(bits), sums)
    homeward(0, out_1, back_1, None)
    other = homeward(1, out_2, back_2, sums)
    total = sums.reshape(16, width // 16)
    step = 1
    while step < groups:
        total = total + lax.ppermute(total, "exp", [(i, i ^ step) for i in range(groups)])
        step *= 2
    total = total.reshape(1, width)
    mixed, grad_tokens = call(
        "tokens",
        functools.partial(token_kernel, capacity),
        [shaped((count, width))] * 2,
        (slot_row, tokens, gain_row, *home),
    )
    total = after(total, grad_tokens)
    grad_gain = (total / gain_row).reshape(width)
    return (mixed, grad_tokens, grad_up[None], grad_down[None], grad_gain)


def solution(mesh):
    return jax.shard_map(
        local,
        mesh=mesh,
        in_specs=(
            P(("rep", "exp"), None),
            P(("rep", "exp"), None),
            P(),
            P("exp", None, "rep"),
            P("exp", "rep", None),
            P(("rep", "exp"), None),
        ),
        out_specs=(
            P(("rep", "exp"), None),
            P(("rep", "exp"), None),
            P("exp", None, "rep"),
            P("exp", "rep", None),
            P(),
        ),
        check_vma=False,
    )
```

```python
import functools

import jax
import jax.numpy as jnp
from jax import lax
from jax.experimental import pallas as pl
from jax.experimental.pallas import tpu as pltpu
from jax.sharding import PartitionSpec as P

gelu_coef = 0.7978845608028654
cubic_coef = 0.044715
bf16 = jnp.bfloat16
f32 = jnp.float32
NN = (((1,), (0,)), ((), ()))
NT = (((1,), (1,)), ((), ()))
TN = (((0,), (0,)), ((), ()))


ROOM = 20 * 1024 * 1024
PLACE_ROOM = 60 * 1024 * 1024


def mm(a, b, dims=NN):
    return lax.dot_general(a, b, dims, preferred_element_type=f32)


def gelu_parts(inputs):
    inner = gelu_coef * (inputs + cubic_coef * inputs * inputs * inputs)
    tangent = jnp.tanh(inner)
    values = 0.5 * inputs * (1.0 + tangent)
    slopes = 0.5 * (1.0 + tangent) + 0.5 * inputs * (1.0 - tangent * tangent) * gelu_coef * (
        1.0 + 3.0 * cubic_coef * inputs * inputs
    )
    return (values, slopes)


def call(name, kernel, out_shape, args, flops=0, moved=0, scratch=(), place=pltpu.VMEM, room=ROOM):
    vmem = pl.BlockSpec(memory_space=pltpu.VMEM)
    return pl.pallas_call(
        kernel,
        name=name,
        out_shape=out_shape,
        in_specs=[pl.BlockSpec(memory_space=place)] * len(args),
        out_specs=jax.tree.map(lambda _: vmem, out_shape),
        scratch_shapes=scratch,
        compiler_params=pltpu.CompilerParams(vmem_limit_bytes=room),
        cost_estimate=pl.CostEstimate(flops=flops, bytes_accessed=moved, transcendentals=0),
    )(*args)


def after(values, *events):
    return lax.optimization_barrier((values, events))[0]


def shaped(shape, dtype=bf16):
    return jax.ShapeDtypeStruct(shape, dtype)


def block_places(slot_row, k, capacity):
    at = slot_row - k * capacity
    return jnp.where((at >= 0) & (at < capacity), at, -2 * capacity)


def place_kernel(groups, capacity, tok_in, id_in, gain_in, cot_in, slot_ref, *refs):
    sends, both, tok_ref, id_ref, gain_ref, sems = refs[:groups], *refs[groups:]
    count = tok_ref.shape[0]
    sources = (id_in, tok_in, gain_in, cot_in)
    targets = (id_ref, tok_ref, gain_ref, both.at[pl.ds(count, count)])
    copies = [pltpu.make_async_copy(a, b, sems.at[i]) for i, (a, b) in enumerate(zip(sources, targets))]
    for copy in copies:
        copy.start()
    copies[0].wait()
    id_row = jnp.broadcast_to(id_ref[...], (count, count))
    id_col = jnp.transpose(id_row)
    at_row = lax.broadcasted_iota(jnp.int32, (count, count), 0)
    at_col = lax.broadcasted_iota(jnp.int32, (count, count), 1)
    earlier = jnp.where((id_row == id_col) & (at_row < at_col), 1, 0)
    ranks = jnp.sum(earlier, axis=0, keepdims=True)
    ahead = id_ref[...] - lax.axis_index("exp").astype(jnp.int32)
    ahead = jnp.where(ahead < 0, ahead + groups, ahead)
    slots = jnp.where(ranks < capacity, ahead * capacity + ranks, -1)
    slot_ref[...] = jnp.where(slots < 0, -2 * groups * capacity, ahead * 2 * capacity + ranks)
    copies[1].wait()
    copies[2].wait()
    wide = tok_ref[...].astype(f32)
    scales = lax.rsqrt(jnp.mean(wide * wide, axis=1, keepdims=True) + 1e-06)
    both[:count] = (wide * scales * gain_ref[...]).astype(bf16)
    copies[3].wait()
    starts = jnp.where(slots < 0, -2 * groups * capacity, ahead * 2 * capacity + ranks)
    wanted = jnp.concatenate([starts, starts + capacity], axis=1)
    step = 2 * capacity
    wide_step = step if step % 8 else groups * step
    for first in range(0, groups * step, wide_step):
        rows = lax.broadcasted_iota(jnp.int32, (wide_step, 2 * count), 0) + first
        found = mm(jnp.where(rows == wanted, 1.0, 0.0).astype(bf16), both[...])
        for at in range(0, wide_step, step):
            sends[(first + at) // step][...] = found[at : at + step].astype(bf16)


def pack_kernel(up_ref, down_ref, pack_ref):
    units = up_ref.shape[1]
    pack_ref[:, :units] = up_ref[...]
    for j in range(up_ref.shape[0] // units):
        at = pl.ds(j * units, units)
        pack_ref[at, units:] = down_ref[:, at]


def hidden_kernel(in_ref, cot_ref, up_a, down_a, pack_b, hid_a, hid_b, pre_a, pre_b):
    width, units = up_a.shape
    step = min(units, 256)
    for i in range(units // step):
        at = pl.ds(i * step, step)
        values, slopes = gelu_parts(mm(in_ref[...], up_a[:, at]))
        hid_a[:, at] = values.astype(bf16)
        pre_a[:, at] = (mm(cot_ref[...], down_a[at, :], NT) * slopes).astype(bf16)
    for i in range(units // step):
        at = pl.ds(i * step, step)
        values, slopes = gelu_parts(mm(in_ref[...], pack_b[:, at]))
        hid_b[:, at] = values.astype(bf16)
        total = None
        for j in range(width // units):
            block = pack_b[pl.ds(j * units + i * step, step), pl.ds(units, units)]
            part = mm(cot_ref[:, pl.ds(j * units, units)], block, NT)
            total = part if total is None else total + part
        pre_b[:, at] = (total * slopes).astype(bf16)


def row_kernel(
    piece, in_ref, hid_a, hid_b, pre_a, pre_b, up_a, down_a, pack_b,
    gain_ref, keep_out, send_out, keep_back, send_back,
):
    rows, width = in_ref.shape
    pieces = rows // piece
    units = up_a.shape[1]
    for i in range(width // 256):
        at = pl.ds(i * 256, 256)
        j, off = divmod(i * 256, units)
        down_b = pack_b[pl.ds(j * units, units), pl.ds(units + off, 256)]
        total = mm(hid_a[...], down_a[:, at]) + mm(hid_b[...], down_b)
        keep_out[:, at] = total[: rows // 2]
        send_out[:, at] = total[rows // 2 :].astype(bf16)
        total = mm(pre_a[...], up_a[at, :], NT) + mm(pre_b[...], pack_b[at, pl.ds(0, units)], NT)
        gain_ref[:, at] = jnp.sum(total * in_ref[:, at].astype(f32), axis=0, keepdims=True)
        for p in range(pieces):
            part = total[p * piece : (p + 1) * piece]
            to = pl.ds((p // 2) * piece, piece)
            if p % 2:
                send_back[to, at] = part.astype(bf16)
            else:
                keep_back[to, at] = part


def grad_kernel(left_a, left_b, right_a, right_b, out_ref, left, right):
    rows = left_a.shape[0]
    left[:rows], left[rows:] = left_a[...], left_b[...]
    right[:rows], right[rows:] = right_a[...], right_b[...]
    for i in range(out_ref.shape[0] // 256):
        at = pl.ds(i * 256, 256)
        out_ref[at, :] = mm(left[:, at], right[...], TN).astype(bf16)


def token_kernel(capacity, slot_ref, tok_ref, gain_ref, *refs):
    blocks, mixed_ref, grad_ref = refs[:-2], refs[-2], refs[-1]
    count = slot_ref.shape[1]
    wanted = jnp.concatenate([slot_ref[...], slot_ref[...] + capacity], axis=1)
    if 2 * capacity % 16:
        parts = [ref[...] for ref in blocks]
    else:
        parts = [jnp.concatenate([ref[...] for ref in blocks], axis=0)]
    found, start = 0.0, 0
    for part in parts:
        rows = lax.broadcasted_iota(jnp.int32, (part.shape[0], 2 * count), 0) + start
        found += mm(jnp.where(rows == wanted, 1.0, 0.0).astype(bf16), part, TN)
        start += part.shape[0]
    mixed, d_normed = found[:count], found[count:]
    mixed_ref[...] = mixed.astype(bf16)
    wide = tok_ref[...].astype(f32)
    scales = lax.rsqrt(jnp.mean(wide * wide, axis=1, keepdims=True) + 1e-06)
    gained = d_normed * gain_ref[...]
    cubed = scales * scales * scales
    grad_ref[...] = (
        scales * gained - wide * (cubed * jnp.mean(gained * wide, axis=1, keepdims=True))
    ).astype(bf16)


def local(tokens, expert_ids, norm_gain, up_weight, down_weight, cotangent):
    groups = lax.axis_size("exp")
    copies = lax.axis_size("rep")
    count, width = tokens.shape
    capacity = 3 * count // (4 * groups)
    piece = groups * capacity // 2
    units = up_weight.shape[2]
    rows = piece * copies // 2
    bits = []
    while (2 << len(bits)) < copies:
        bits.append(2 << len(bits))

    def swap(x, bit):
        return lax.ppermute(x, "rep", [(i, i ^ bit) for i in range(copies)])

    def shift(x, k):
        return lax.ppermute(x, "exp", [(i, (i + k) % groups) for i in range(groups)])

    def join(*arrays):
        return jnp.concatenate(arrays, axis=0)

    up_a, down_a = up_weight[0], down_weight[0]

    gain_row = norm_gain.reshape(1, width)
    slot_row, *blocks = call(
        "place",
        functools.partial(place_kernel, groups, capacity),
        [shaped((1, count), jnp.int32)] + [shaped((2 * capacity, width))] * groups,
        (tokens, expert_ids.reshape(1, count), gain_row, cotangent),
        scratch=[
            pltpu.VMEM((2 * count, width), bf16),
            pltpu.VMEM((count, width), bf16),
            pltpu.VMEM((1, count), jnp.int32),
            pltpu.VMEM((1, width), f32),
            pltpu.SemaphoreType.DMA((4,)),
        ],
        place=pltpu.HBM,
        room=PLACE_ROOM,
    )
    pack_a = call(
        "pack",
        pack_kernel,
        shaped((width, 2 * units)),
        after((up_a, down_a), blocks[0]),
        2,
        8 << 20,
    )
    pack_b = swap(pack_a, 1)
    early = groups // 2
    arrived = [blocks[0]] + [shift(blocks[k], k) for k in range(1, early)]
    blocks = after(blocks, arrived[1:])
    arrived.append(shift(blocks[early], early))

    def start(n):
        mine = [arrived[k] for k in range(n * groups // 2, (n + 1) * groups // 2)]
        return [{0: join(*[block[:capacity] for block in mine])}, {0: join(*[block[capacity:] for block in mine])}]

    def ordered(held):
        return join(*[held[at] for at in sorted(held)])

    def grow(held, bit):
        known = sorted(held)
        got = swap(ordered(held), bit)
        return {**held, **{at ^ bit: got[n * piece : (n + 1) * piece] for n, at in enumerate(known)}}

    def halved(x, first):
        cut = x.shape[0] // 2
        if first:
            x = x.reshape(-1, 2, piece, width)
            return x[:, 0].reshape(cut, width), x[:, 1].reshape(cut, width)
        return x[:cut], x[cut:]

    down_bits = list(reversed(bits))
    work = 8 * rows * width * 2 * units
    weights = (up_a, down_a, pack_b)

    def gather(pair, events):
        for n, (bit, back_bit) in enumerate(zip(bits, down_bits)):
            pair = after(pair, *events[n]) if n in events else pair
            pair = [grow(pair[0], bit), grow(pair[1], back_bit)]
            yield pair

    def hidden(in_rows, cot_rows):
        return call(
            "hidden",
            hidden_kernel,
            [shaped((rows, units))] * 4,
            (in_rows, cot_rows, *weights),
            work // 2,
            8 << 20,
        )

    def products(in_rows, acts):
        kept = [shaped((rows // 2, width), f32), shaped((rows // 2, width))] * 2
        return call(
            "rows",
            functools.partial(row_kernel, piece),
            [shaped((1, width), f32)] + kept,
            (in_rows, *acts, *weights),
            work // 2,
            8 << 20,
        )

    def packed(sums):
        lead = lax.reduce_precision(sums, 8, 7)
        return jnp.pad(join(lead, sums - lead), ((0, 6), (0, 0))).astype(bf16)

    def unpacked(pair):
        return pair[0:1].astype(f32) + pair[1:2].astype(f32)

    def scatter(parts, events, sums=None):
        out, back = parts[1:3], parts[3:5]
        for n, (bit, back_bit) in enumerate(zip(down_bits, bits)):
            sent = back[1] if sums is None else join(back[1], packed(sums))
            got_out, got_back = after((swap(out[1], bit), swap(sent, back_bit)), *events[n])
            if sums is not None:
                sums = sums + unpacked(got_back[-8:])
                got_back = got_back[:-8]
            out, back = out[0] + got_out.astype(f32), back[0] + got_back.astype(f32)
            if n < len(bits) - 1:
                out, back = halved(out, False), halved(back, True)
                out, back = (out[0], out[1].astype(bf16)), (back[0], back[1].astype(bf16))
        return out.astype(bf16), back.astype(bf16), sums

    def homeward(n, out_rows, back_rows, sums):
        other = []
        for i in range(groups // 2):
            k = n * groups // 2 + i
            cut = slice(i * capacity, (i + 1) * capacity)
            block = join(out_rows[cut], back_rows[cut])
            if k and sums is not None:
                home[k] = shift(block, groups - k)
            else:
                home[k] = shift(block, groups - k) if k else block
        return other

    steps = list(gather(start(0), {}))
    in_1, cot_1 = [ordered(held) for held in steps[-1]]
    acts_1 = hidden(in_1, cot_1)
    events = [ordered(held) for held in steps[0]]
    arrived += [shift(after(blocks[k], events[1]), k) for k in range(early + 1, groups)]
    steps = list(gather(start(1), {0: [ordered(held) for held in steps[0]], len(bits) - 1: (acts_1,)}))
    parts_1 = products(after(in_1, steps[-2]), acts_1)
    in_2, cot_2 = [ordered(held) for held in after(steps[-1], parts_1)]
    acts_2 = hidden(in_2, cot_2)
    parts_2 = products(in_2, acts_2)
    in_all, cot_all = join(in_1, in_2), join(cot_1, cot_2)
    hid_a, hid_b, pre_a, pre_b = [join(a, b) for a, b in zip(acts_1, acts_2)]
    wide_rows = pltpu.VMEM((4 * rows, width), bf16)
    unit_rows = pltpu.VMEM((4 * rows, units), bf16)
    grad_down = call(
        "grad_down",
        grad_kernel,
        shaped((units, width)),
        (hid_a, swap(hid_b, 1), cot_all, swap(cot_all, 1)),
        work // 4,
        8 << 20,
        [unit_rows, wide_rows],
    )
    grad_up = call(
        "grad_up",
        grad_kernel,
        shaped((width, units)),
        (in_all, swap(in_all, 1), pre_a, swap(pre_b, 1)),
        work // 4,
        8 << 20,
        [wide_rows, unit_rows],
    )
    home = [None] * groups
    sums = parts_1[0] + parts_2[0]
    sums = sums + swap(sums, 1)
    out_1, back_1, _ = scatter(parts_1, [(sums,)] + [(grad_down,)] * len(bits))
    out_2, back_2, sums = scatter(parts_2, [(grad_up,)] + [()] * len(bits), sums)
    homeward(0, out_1, back_1, None)
    other = homeward(1, out_2, back_2, sums)
    total = sums.reshape(16, width // 16)
    step = 1
    while step < groups:
        total = total + lax.ppermute(total, "exp", [(i, i ^ step) for i in range(groups)])
        step *= 2
    total = total.reshape(1, width)
    mixed, grad_tokens = call(
        "tokens",
        functools.partial(token_kernel, capacity),
        [shaped((count, width))] * 2,
        (slot_row, tokens, gain_row, *home),
    )
    total = after(total, grad_tokens)
    grad_gain = (total / gain_row).reshape(width)
    return (mixed, grad_tokens, grad_up[None], grad_down[None], grad_gain)


def solution(mesh):
    return jax.shard_map(
        local,
        mesh=mesh,
        in_specs=(
            P(("rep", "exp"), None),
            P(("rep", "exp"), None),
            P(),
            P("exp", None, "rep"),
            P("exp", "rep", None),
            P(("rep", "exp"), None),
        ),
        out_specs=(
            P(("rep", "exp"), None),
            P(("rep", "exp"), None),
            P("exp", None, "rep"),
            P("exp", "rep", None),
            P(),
        ),
        check_vma=False,
    )
```

```python
import functools

import jax
import jax.numpy as jnp
from jax import lax
from jax.experimental import pallas as pl
from jax.experimental.pallas import tpu as pltpu
from jax.sharding import PartitionSpec as P

gelu_coef = 0.7978845608028654
cubic_coef = 0.044715
bf16 = jnp.bfloat16
f32 = jnp.float32
NN = (((1,), (0,)), ((), ()))
NT = (((1,), (1,)), ((), ()))
TN = (((0,), (0,)), ((), ()))


ROOM = 20 * 1024 * 1024
PLACE_ROOM = 60 * 1024 * 1024


def mm(a, b, dims=NN):
    return lax.dot_general(a, b, dims, preferred_element_type=f32)


def gelu_parts(inputs):
    inner = gelu_coef * (inputs + cubic_coef * inputs * inputs * inputs)
    tangent = jnp.tanh(inner)
    values = 0.5 * inputs * (1.0 + tangent)
    slopes = 0.5 * (1.0 + tangent) + 0.5 * inputs * (1.0 - tangent * tangent) * gelu_coef * (
        1.0 + 3.0 * cubic_coef * inputs * inputs
    )
    return (values, slopes)


def call(name, kernel, out_shape, args, flops=0, moved=0, scratch=(), place=pltpu.VMEM, room=ROOM):
    vmem = pl.BlockSpec(memory_space=pltpu.VMEM)
    return pl.pallas_call(
        kernel,
        name=name,
        out_shape=out_shape,
        in_specs=[pl.BlockSpec(memory_space=place)] * len(args),
        out_specs=jax.tree.map(lambda _: vmem, out_shape),
        scratch_shapes=scratch,
        compiler_params=pltpu.CompilerParams(vmem_limit_bytes=room),
        cost_estimate=pl.CostEstimate(flops=flops, bytes_accessed=moved, transcendentals=0),
    )(*args)


def after(values, *events):
    return lax.optimization_barrier((values, events))[0]


def shaped(shape, dtype=bf16):
    return jax.ShapeDtypeStruct(shape, dtype)


def block_places(slot_row, k, capacity):
    at = slot_row - k * capacity
    return jnp.where((at >= 0) & (at < capacity), at, -2 * capacity)


def place_kernel(groups, capacity, tok_in, id_in, gain_in, cot_in, slot_ref, *refs):
    sends, both, tok_ref, id_ref, gain_ref, sems = refs[:groups], *refs[groups:]
    count = tok_ref.shape[0]
    sources = (id_in, tok_in, gain_in, cot_in)
    targets = (id_ref, tok_ref, gain_ref, both.at[pl.ds(count, count)])
    copies = [pltpu.make_async_copy(a, b, sems.at[i]) for i, (a, b) in enumerate(zip(sources, targets))]
    for copy in copies:
        copy.start()
    copies[0].wait()
    id_row = jnp.broadcast_to(id_ref[...], (count, count))
    id_col = jnp.transpose(id_row)
    at_row = lax.broadcasted_iota(jnp.int32, (count, count), 0)
    at_col = lax.broadcasted_iota(jnp.int32, (count, count), 1)
    earlier = jnp.where((id_row == id_col) & (at_row < at_col), 1, 0)
    ranks = jnp.sum(earlier, axis=0, keepdims=True)
    ahead = id_ref[...] - lax.axis_index("exp").astype(jnp.int32)
    ahead = jnp.where(ahead < 0, ahead + groups, ahead)
    slots = jnp.where(ranks < capacity, ahead * capacity + ranks, -1)
    slot_ref[...] = jnp.where(slots < 0, -2 * groups * capacity, ahead * 2 * capacity + ranks)
    copies[1].wait()
    copies[2].wait()
    wide = tok_ref[...].astype(f32)
    scales = lax.rsqrt(jnp.mean(wide * wide, axis=1, keepdims=True) + 1e-06)
    both[:count] = (wide * scales * gain_ref[...]).astype(bf16)
    copies[3].wait()
    starts = jnp.where(slots < 0, -2 * groups * capacity, ahead * 2 * capacity + ranks)
    wanted = jnp.concatenate([starts, starts + capacity], axis=1)
    step = 2 * capacity
    wide_step = step if step % 8 else groups * step
    for first in range(0, groups * step, wide_step):
        rows = lax.broadcasted_iota(jnp.int32, (wide_step, 2 * count), 0) + first
        found = mm(jnp.where(rows == wanted, 1.0, 0.0).astype(bf16), both[...])
        for at in range(0, wide_step, step):
            sends[(first + at) // step][...] = found[at : at + step].astype(bf16)


def pack_kernel(up_ref, down_ref, pack_ref):
    units = up_ref.shape[1]
    pack_ref[:, :units] = up_ref[...]
    for j in range(up_ref.shape[0] // units):
        at = pl.ds(j * units, units)
        pack_ref[at, units:] = down_ref[:, at]


def hidden_kernel(in_ref, cot_ref, up_a, down_a, pack_b, hid_a, hid_b, pre_a, pre_b):
    width, units = up_a.shape
    step = min(units, 256)
    for i in range(units // step):
        at = pl.ds(i * step, step)
        values, slopes = gelu_parts(mm(in_ref[...], up_a[:, at]))
        hid_a[:, at] = values.astype(bf16)
        pre_a[:, at] = (mm(cot_ref[...], down_a[at, :], NT) * slopes).astype(bf16)
    for i in range(units // step):
        at = pl.ds(i * step, step)
        values, slopes = gelu_parts(mm(in_ref[...], pack_b[:, at]))
        hid_b[:, at] = values.astype(bf16)
        total = None
        for j in range(width // units):
            block = pack_b[pl.ds(j * units + i * step, step), pl.ds(units, units)]
            part = mm(cot_ref[:, pl.ds(j * units, units)], block, NT)
            total = part if total is None else total + part
        pre_b[:, at] = (total * slopes).astype(bf16)


def row_kernel(
    piece, in_ref, hid_a, hid_b, pre_a, pre_b, up_a, down_a, pack_b,
    gain_ref, keep_out, send_out, keep_back, send_back,
):
    rows, width = in_ref.shape
    pieces = rows // piece
    units = up_a.shape[1]
    for i in range(width // 256):
        at = pl.ds(i * 256, 256)
        j, off = divmod(i * 256, units)
        down_b = pack_b[pl.ds(j * units, units), pl.ds(units + off, 256)]
        total = mm(hid_a[...], down_a[:, at]) + mm(hid_b[...], down_b)
        keep_out[:, at] = total[: rows // 2]
        send_out[:, at] = total[rows // 2 :].astype(bf16)
        total = mm(pre_a[...], up_a[at, :], NT) + mm(pre_b[...], pack_b[at, pl.ds(0, units)], NT)
        gain_ref[:, at] = jnp.sum(total * in_ref[:, at].astype(f32), axis=0, keepdims=True)
        for p in range(pieces):
            part = total[p * piece : (p + 1) * piece]
            to = pl.ds((p // 2) * piece, piece)
            if p % 2:
                send_back[to, at] = part.astype(bf16)
            else:
                keep_back[to, at] = part


def grad_kernel(starts, left_a, left_b, right_a, right_b, out_ref, left, right):
    rows = left_a.shape[0]
    left[:rows], left[rows:] = left_a[...], left_b[pl.ds(starts[0], rows)]
    right[:rows], right[rows:] = right_a[...], right_b[pl.ds(starts[1], rows)]
    for i in range(out_ref.shape[0] // 256):
        at = pl.ds(i * 256, 256)
        out_ref[at, :] = mm(left[:, at], right[...], TN).astype(bf16)


def token_kernel(capacity, slot_ref, tok_ref, gain_ref, *refs):
    blocks, mixed_ref, grad_ref = refs[:-2], refs[-2], refs[-1]
    count = slot_ref.shape[1]
    wanted = jnp.concatenate([slot_ref[...], slot_ref[...] + capacity], axis=1)
    if 2 * capacity % 16:
        parts = [ref[...] for ref in blocks]
    else:
        parts = [jnp.concatenate([ref[...] for ref in blocks], axis=0)]
    found, start = 0.0, 0
    for part in parts:
        rows = lax.broadcasted_iota(jnp.int32, (part.shape[0], 2 * count), 0) + start
        found += mm(jnp.where(rows == wanted, 1.0, 0.0).astype(bf16), part, TN)
        start += part.shape[0]
    mixed, d_normed = found[:count], found[count:]
    mixed_ref[...] = mixed.astype(bf16)
    wide = tok_ref[...].astype(f32)
    scales = lax.rsqrt(jnp.mean(wide * wide, axis=1, keepdims=True) + 1e-06)
    gained = d_normed * gain_ref[...]
    cubed = scales * scales * scales
    grad_ref[...] = (
        scales * gained - wide * (cubed * jnp.mean(gained * wide, axis=1, keepdims=True))
    ).astype(bf16)


def local(tokens, expert_ids, norm_gain, up_weight, down_weight, cotangent):
    groups = lax.axis_size("exp")
    copies = lax.axis_size("rep")
    count, width = tokens.shape
    capacity = 3 * count // (4 * groups)
    piece = groups * capacity // 2
    units = up_weight.shape[2]
    rows = piece * copies // 2
    bits = []
    while (2 << len(bits)) < copies:
        bits.append(2 << len(bits))

    def swap(x, bit):
        return lax.ppermute(x, "rep", [(i, i ^ bit) for i in range(copies)])

    def shift(x, k):
        return lax.ppermute(x, "exp", [(i, (i + k) % groups) for i in range(groups)])

    def join(*arrays):
        return jnp.concatenate(arrays, axis=0)

    up_a, down_a = up_weight[0], down_weight[0]

    gain_row = norm_gain.reshape(1, width)
    slot_row, *blocks = call(
        "place",
        functools.partial(place_kernel, groups, capacity),
        [shaped((1, count), jnp.int32)] + [shaped((2 * capacity, width))] * groups,
        (tokens, expert_ids.reshape(1, count), gain_row, cotangent),
        scratch=[
            pltpu.VMEM((2 * count, width), bf16),
            pltpu.VMEM((count, width), bf16),
            pltpu.VMEM((1, count), jnp.int32),
            pltpu.VMEM((1, width), f32),
            pltpu.SemaphoreType.DMA((4,)),
        ],
        place=pltpu.HBM,
        room=PLACE_ROOM,
    )
    pack_a = call(
        "pack",
        pack_kernel,
        shaped((width, 2 * units)),
        after((up_a, down_a), blocks[0]),
        2,
        8 << 20,
    )
    pack_b = swap(pack_a, 1)
    early = groups // 2
    arrived = [blocks[0]] + [shift(blocks[k], k) for k in range(1, early)]
    blocks = after(blocks, arrived[1:])
    arrived.append(shift(blocks[early], early))

    def start(n):
        mine = [arrived[k] for k in range(n * groups // 2, (n + 1) * groups // 2)]
        return [{0: join(*[block[:capacity] for block in mine])}, {0: join(*[block[capacity:] for block in mine])}]

    def ordered(held):
        return join(*[held[at] for at in sorted(held)])

    def grow(held, bit):
        known = sorted(held)
        got = swap(ordered(held), bit)
        return {**held, **{at ^ bit: got[n * piece : (n + 1) * piece] for n, at in enumerate(known)}}

    def halved(x, first):
        cut = x.shape[0] // 2
        if first:
            x = x.reshape(-1, 2, piece, width)
            return x[:, 0].reshape(cut, width), x[:, 1].reshape(cut, width)
        return x[:cut], x[cut:]

    down_bits = list(reversed(bits))
    work = 8 * rows * width * 2 * units
    weights = (up_a, down_a, pack_b)

    def gather(pair, events):
        for n, (bit, back_bit) in enumerate(zip(bits, down_bits)):
            pair = after(pair, *events[n]) if n in events else pair
            pair = [grow(pair[0], bit), grow(pair[1], back_bit)]
            yield pair

    def hidden(in_rows, cot_rows):
        return call(
            "hidden",
            hidden_kernel,
            [shaped((rows, units))] * 4,
            (in_rows, cot_rows, *weights),
            work // 2,
            8 << 20,
        )

    def products(in_rows, acts):
        kept = [shaped((rows // 2, width), f32), shaped((rows // 2, width))] * 2
        return call(
            "rows",
            functools.partial(row_kernel, piece),
            [shaped((1, width), f32)] + kept,
            (in_rows, *acts, *weights),
            work // 2,
            8 << 20,
        )

    def packed(sums):
        lead = lax.reduce_precision(sums, 8, 7)
        return jnp.pad(join(lead, sums - lead), ((0, 6), (0, 0))).astype(bf16)

    def unpacked(pair):
        return pair[0:1].astype(f32) + pair[1:2].astype(f32)

    def scatter(parts, events, sums=None):
        out, back = parts[1:3], parts[3:5]
        for n, (bit, back_bit) in enumerate(zip(down_bits, bits)):
            sent = back[1] if sums is None else join(back[1], packed(sums))
            got_out, got_back = after((swap(out[1], bit), swap(sent, back_bit)), *events[n])
            if sums is not None:
                sums = sums + unpacked(got_back[-8:])
                got_back = got_back[:-8]
            out, back = out[0] + got_out.astype(f32), back[0] + got_back.astype(f32)
            if n < len(bits) - 1:
                out, back = halved(out, False), halved(back, True)
                out, back = (out[0], out[1].astype(bf16)), (back[0], back[1].astype(bf16))
        return out.astype(bf16), back.astype(bf16), sums

    def homeward(n, out_rows, back_rows, sums):
        other = []
        for i in range(groups // 2):
            k = n * groups // 2 + i
            cut = slice(i * capacity, (i + 1) * capacity)
            block = join(out_rows[cut], back_rows[cut])
            if k and sums is not None:
                home[k] = shift(block, groups - k)
            else:
                home[k] = shift(block, groups - k) if k else block
        return other

    steps = list(gather(start(0), {}))
    in_1, cot_1 = [ordered(held) for held in steps[-1]]
    acts_1 = hidden(in_1, cot_1)
    events = [ordered(held) for held in steps[0]]
    arrived += [shift(after(blocks[k], events[1]), k) for k in range(early + 1, groups)]
    steps = list(gather(start(1), {0: [ordered(held) for held in steps[0]], len(bits) - 1: (acts_1,)}))
    parts_1 = products(after(in_1, steps[-2]), acts_1)
    in_2, cot_2 = [ordered(held) for held in after(steps[-1], parts_1)]
    acts_2 = hidden(in_2, cot_2)
    parts_2 = products(in_2, acts_2)
    in_all, cot_all = join(in_1, in_2), join(cot_1, cot_2)
    hid_a, hid_b, pre_a, pre_b = [join(a, b) for a, b in zip(acts_1, acts_2)]
    wide_rows = pltpu.VMEM((4 * rows, width), bf16)
    unit_rows = pltpu.VMEM((4 * rows, units), bf16)
    units_got = swap(join(hid_b, pre_b), 1)
    grad_down = call(
        "grad_down",
        functools.partial(grad_kernel, (0, 0)),
        shaped((units, width)),
        (hid_a, units_got, cot_all, swap(cot_all, 1)),
        work // 4,
        8 << 20,
        [unit_rows, wide_rows],
    )
    grad_up = call(
        "grad_up",
        functools.partial(grad_kernel, (0, 2 * rows)),
        shaped((width, units)),
        (in_all, swap(in_all, 1), pre_a, units_got),
        work // 4,
        8 << 20,
        [wide_rows, unit_rows],
    )
    home = [None] * groups
    sums = parts_1[0] + parts_2[0]
    sums = sums + swap(sums, 1)
    out_1, back_1, _ = scatter(parts_1, [(sums,)] + [(grad_down,)] * len(bits))
    out_2, back_2, sums = scatter(parts_2, [(grad_up,)] + [()] * len(bits), sums)
    homeward(0, out_1, back_1, None)
    other = homeward(1, out_2, back_2, sums)
    total = sums.reshape(16, width // 16)
    step = 1
    while step < groups:
        total = total + lax.ppermute(total, "exp", [(i, i ^ step) for i in range(groups)])
        step *= 2
    total = total.reshape(1, width)
    mixed, grad_tokens = call(
        "tokens",
        functools.partial(token_kernel, capacity),
        [shaped((count, width))] * 2,
        (slot_row, tokens, gain_row, *home),
    )
    total = after(total, grad_tokens)
    grad_gain = (total / gain_row).reshape(width)
    return (mixed, grad_tokens, grad_up[None], grad_down[None], grad_gain)


def solution(mesh):
    return jax.shard_map(
        local,
        mesh=mesh,
        in_specs=(
            P(("rep", "exp"), None),
            P(("rep", "exp"), None),
            P(),
            P("exp", None, "rep"),
            P("exp", "rep", None),
            P(("rep", "exp"), None),
        ),
        out_specs=(
            P(("rep", "exp"), None),
            P(("rep", "exp"), None),
            P("exp", None, "rep"),
            P("exp", "rep", None),
            P(),
        ),
        check_vma=False,
    )
```
